32 devices in a mesh: segment: 8 (over z, x), dp: 4 (over y, core).
Axes of the slice: x: 2, y: 2, z: 4, core: 2. Of those that a mesh axis runs over, the one named last changes fastest.
Arguments:
- checkpoint: bfloat16 [8, 2, 4, 16, 16, 1024], P('segment', None, 'dp'), may hold values from -6 to 6
- cotangent: bfloat16 [2, 4, 16, 16, 1024], P(None, 'dp'), may hold values from -6 to 6
- depthwise: float32 [8, 2, 25, 1024], P('segment'), may hold values from -1.8 to 1.8
- pointwise: bfloat16 [8, 1024, 2, 1024], P('segment', 'dp'), may hold values from -0.1875 to 0.1875
- genotype: int32 [8], P('segment'), may hold values from 0 to 2, as said below
Outputs:
- grad_input: bfloat16 [8, 2, 4, 16, 16, 1024], P('segment', None, 'dp')
- grad_point: float32 [8, 1024, 2, 1024], P('segment', 'dp')
- grad_depth: float32 [8, 2, 25, 1024], P('segment')
The draws below stay inside these ranges and needn't reach their ends.
Inputs may be any that keep to these rules, and one draw needn't show every extreme that they name: `genotype`: 0 separable 3x3, 1 separable 5x5, 2 dilated separable 3x3; both 0 and 2 occur.
All inputs are finite; a program needn't handle non-finite values.
Results may differ from the reference program's by a relative error of at most 0.025.
Values may be sent and summed in bfloat16 or wider, within the bound.
No kernel may reach another device: no remote copies, remote signals or barrier semaphores. Data moves between devices by JAX's collectives and lax.ppermute only.
A program may use at most 128 MiB of HBM per device.

```python
import jax
import jax.numpy as jnp
from jax import lax

C = 1024
TAPS = 25
SIDE = 16
MICRO = 2
IMAGES = 4
SEGMENTS = 8


def draw_genotype(key, part):
    key_vals, key_first, key_second = jax.random.split(key, 3)
    values = jax.random.randint(key_vals, (SEGMENTS,), 0, 3)
    place_two = jax.random.randint(key_first, (), 0, SEGMENTS)
    place_zero = (place_two + 1 + jax.random.randint(key_second, (), 0, SEGMENTS - 1)) % SEGMENTS
    positions = jnp.arange(SEGMENTS)
    values = jnp.where(positions == place_two, 2, values)
    values = jnp.where(positions == place_zero, 0, values)
    return values.astype(jnp.int32)


def shard_levels(rng, dims, pieces, smallest, largest):
    def one(axis_at, shards_of):
        draws = jax.random.uniform(jax.random.fold_in(jax.random.fold_in(rng, 6), axis_at), (shards_of,), jnp.float32, smallest / len(pieces), largest / len(pieces))
        return jnp.repeat(jnp.exp(draws), dims[axis_at] // shards_of).reshape((-1,) + (1,) * (len(dims) - axis_at - 1))

    loudness = one(*pieces[0])
    for cut in pieces[1:]:
        loudness = loudness * one(*cut)
    return loudness


def scatter_about(key, shape, width, bound, cuts=(), held_as=jnp.bfloat16):
    array = jax.random.normal(key, shape, jnp.float32) * width
    if len(cuts) > 0:
        array = shard_levels(key, shape, cuts, -0.22, 0.18) * array
    return jnp.clip(array, min=-bound, max=bound).astype(held_as)


def setup_inputs(seed: int = 0) -> dict:
    seeds = jax.random.split(jax.random.key(seed), 6)
    return {
        "checkpoint": scatter_about(seeds[0], (SEGMENTS, MICRO, IMAGES, SIDE, SIDE, C), 1.0, 6.0, ((0, 8), (2, 4))),
        "cotangent": scatter_about(seeds[1], (MICRO, IMAGES, SIDE, SIDE, C), 1.0, 6.0, ((1, 4),)),
        "depthwise": scatter_about(seeds[2], (SEGMENTS, 2, TAPS, C), 0.3, 1.8, ((0, 8),), jnp.float32),
        "pointwise": scatter_about(seeds[3], (SEGMENTS, C, 2, C), C ** -0.5, 0.1875, ((0, 8), (1, 4))),
        "genotype": draw_genotype(jax.random.fold_in(seeds[5], 71), 0),
    }


def tap_mask(operation):
    tap_ids = jnp.arange(25, dtype=jnp.int32)
    row_off = tap_ids // 5 - 2
    col_off = tap_ids % 5 - 2
    narrow = (jnp.abs(row_off) <= 1) & (jnp.abs(col_off) <= 1)
    dilated = (row_off % 2 == 0) & (col_off % 2 == 0)
    kept_taps = jnp.where(operation == 0, narrow, jnp.where(operation == 1, True, dilated))
    return kept_taps.astype(jnp.float32)

def spread(values, kernel):
    grid_side = values.shape[1]
    padded = jnp.pad(values.astype(jnp.float32), ((0, 0), (2, 2), (2, 2), (0, 0)))
    running = jnp.zeros(values.shape, jnp.float32)
    for tap_number in range(25):
        tap_row, tap_col = divmod(tap_number, 5)
        running = running + kernel[tap_number] * padded[:, tap_row:tap_row + grid_side, tap_col:tap_col + grid_side, :]
    return running

def spread_back(gradient, kernel):
    grid_side = gradient.shape[1]
    padded = jnp.pad(gradient, ((0, 0), (2, 2), (2, 2), (0, 0)))
    running = jnp.zeros(gradient.shape, jnp.float32)
    for tap_number in range(25):
        tap_row, tap_col = divmod(tap_number, 5)
        running = running + kernel[tap_number] * padded[:, 4 - tap_row:4 - tap_row + grid_side, 4 - tap_col:4 - tap_col + grid_side, :]
    return running

def kernel_grad(values, gradient):
    grid_side = values.shape[1]
    padded = jnp.pad(values.astype(jnp.float32), ((0, 0), (2, 2), (2, 2), (0, 0)))
    columns = []
    for tap_number in range(25):
        tap_row, tap_col = divmod(tap_number, 5)
        window = padded[:, tap_row:tap_row + grid_side, tap_col:tap_col + grid_side, :]
        columns.append(lax.optimization_barrier(jnp.sum(window * gradient, axis=(0, 1, 2))))
    return jnp.stack(columns, 0)

def segment_backward(x_segment, upstream, depth_segment, panel, operation):
    tap_keep = tap_mask(operation)
    k_first = depth_segment[0] * tap_keep[:, None]
    k_second = depth_segment[1] * tap_keep[:, None]
    grid_shape = (MICRO * IMAGES, SIDE, SIDE, C)
    x_grid = x_segment.reshape(grid_shape)
    activated = jnp.maximum(x_grid, 0)
    first = spread(activated, k_first).astype(jnp.bfloat16)
    first_flat = first.reshape(-1, C)
    pre_act = jnp.dot(first_flat, panel[:, 0, :], preferred_element_type=jnp.float32)
    hidden = jax.nn.silu(pre_act).astype(jnp.bfloat16)
    mixed = spread(hidden.reshape(grid_shape), k_second).astype(jnp.bfloat16)
    up_flat = upstream.reshape(-1, C)
    grad_mix = jnp.dot(up_flat, panel[:, 1, :].T, preferred_element_type=jnp.float32)
    sigma = jax.nn.sigmoid(pre_act)
    slope = sigma * (1.0 + pre_act * (1.0 - sigma))
    grad_pre = (spread_back(grad_mix.reshape(grid_shape), k_second).reshape(-1, C) * slope).astype(jnp.bfloat16)
    grad_lin = jnp.dot(grad_pre, panel[:, 0, :].T, preferred_element_type=jnp.float32)
    grad_in = (upstream.reshape(grid_shape).astype(jnp.float32) + spread_back(grad_lin.reshape(grid_shape), k_first) * (x_grid > 0)).astype(jnp.bfloat16)
    w_grad = jnp.stack([jnp.dot(first_flat.T, grad_pre, preferred_element_type=jnp.float32), jnp.dot(mixed.reshape(-1, C).T, up_flat, preferred_element_type=jnp.float32)], 1)
    k_grad = jnp.stack([kernel_grad(activated, grad_lin.reshape(grid_shape)) * tap_keep[:, None], kernel_grad(hidden.reshape(grid_shape), grad_mix.reshape(grid_shape)) * tap_keep[:, None]], 0)
    return (grad_in.reshape(upstream.shape), w_grad, k_grad)

def reference(checkpoint, cotangent, depthwise, pointwise, genotype):
    mean_scale = 1.0 / (MICRO * IMAGES)

    def carried(upstream, segment_pack):
        x_segment, depth_segment, panel, operation = segment_pack
        grad_in, w_grad, k_grad = segment_backward(x_segment, upstream, depth_segment, panel, operation)
        return (grad_in, (grad_in, w_grad * mean_scale, k_grad * mean_scale))
    unused, outputs = lax.scan(carried, cotangent, (checkpoint, depthwise, pointwise, genotype), reverse=True)
    return (outputs[0], outputs[1], outputs[2])
```

```python
import jax
import jax.numpy as jnp
from jax import lax
from jax.sharding import PartitionSpec as P


def swap(value, axis, bit):
    count = lax.axis_size(axis)
    return lax.ppermute(value, axis, [(source, source ^ bit) for source in range(count)])


def tap_mask(operation):
    tap_ids = jnp.arange(25, dtype=jnp.int32)
    row_off = tap_ids // 5 - 2
    col_off = tap_ids % 5 - 2
    narrow = (jnp.abs(row_off) <= 1) & (jnp.abs(col_off) <= 1)
    dilated = (row_off % 2 == 0) & (col_off % 2 == 0)
    kept_taps = jnp.where(operation == 0, narrow, jnp.where(operation == 1, True, dilated))
    return kept_taps.astype(jnp.float32)


def spread(values, kernel):
    side = values.shape[1]
    padded = jnp.pad(values.astype(jnp.float32), ((0, 0), (2, 2), (2, 2), (0, 0)))
    running = jnp.zeros(values.shape, jnp.float32)
    for tap in range(25):
        row, col = divmod(tap, 5)
        running = running + kernel[tap] * padded[:, row : row + side, col : col + side, :]
    return running


def kernel_grad(values, gradient):
    side = values.shape[1]
    padded = jnp.pad(values.astype(jnp.float32), ((0, 0), (2, 2), (2, 2), (0, 0)))
    gradient = gradient.astype(jnp.float32)
    columns = []
    for tap in range(25):
        row, col = divmod(tap, 5)
        window = padded[:, row : row + side, col : col + side, :]
        columns.append(jnp.sum(window * gradient, axis=(0, 1, 2)))
    return jnp.stack(columns, 0)


def times(left, right):
    return jnp.dot(left, right, preferred_element_type=jnp.float32)


def times_transposed(left, right):
    return lax.dot_general(
        left, right, (((1,), (1,)), ((), ())), preferred_element_type=jnp.float32
    )


def inner_rows(left, right):
    return lax.dot_general(
        left, right, (((0,), (0,)), ((), ())), preferred_element_type=jnp.float32
    )


def forward(x_rows, kernels, w_first, grid):
    act = jnp.maximum(x_rows, 0).reshape(grid)
    first = spread(act, kernels[0]).astype(jnp.bfloat16).reshape(x_rows.shape)
    pre_act = times(first, w_first)
    sigma = jax.nn.sigmoid(pre_act)
    hidden = (pre_act * sigma).astype(jnp.bfloat16)
    slope = (sigma * (1.0 + pre_act * (1.0 - sigma))).astype(jnp.bfloat16)
    mixed = spread(hidden.reshape(grid), kernels[1]).astype(jnp.bfloat16).reshape(x_rows.shape)
    return first, hidden, slope, mixed


def backward(upstream, x_rows, slope, kernels, w_first, w_second, grid):
    flipped = kernels[:, ::-1]
    grad_mix = times_transposed(upstream, w_second)
    back = spread(grad_mix.reshape(grid), flipped[1]).reshape(upstream.shape)
    grad_pre = (back * slope).astype(jnp.bfloat16)
    grad_lin = times_transposed(grad_pre, w_first)
    back = spread(grad_lin.reshape(grid), flipped[0]).reshape(upstream.shape)
    grad_in = (upstream.astype(jnp.float32) + back * (x_rows > 0)).astype(jnp.bfloat16)
    return grad_in, grad_pre, grad_mix.astype(jnp.bfloat16), grad_lin.astype(jnp.bfloat16)


def body(checkpoint, cotangent, depthwise, pointwise, genotype):
    micro, images, side = checkpoint.shape[1:4]
    channels = checkpoint.shape[5]
    rows = images * side * side
    grid = (images, side, side, channels)
    dp = lax.axis_size("dp")
    sections = lax.axis_size("segment")
    pairs = sections // 2
    segment = lax.axis_index("segment")
    data = lax.axis_index("dp")
    half = segment % 2
    pair = segment // 2
    is_high = half == 1
    share = channels // dp
    mean_scale = 1.0 / (micro * images * dp)

    own = jnp.swapaxes(pointwise[0], 0, 1)
    panels = jnp.zeros((2, 2, channels, channels), jnp.bfloat16)

    def keep(panels, piece, section, conv, index):
        return lax.dynamic_update_slice(
            panels, piece[None, None], (section, conv, index * share, 0)
        )

    held = []
    for conv in range(2):
        held.append((half, conv, own[conv]))
    for conv in range(2):
        held.append((1 - half, conv, swap(own[conv], "segment", 1)))
    for section, conv, piece in held:
        got = [(0, piece)]
        bit = dp // 2
        while bit >= 1:
            got = got + [(mask ^ bit, swap(part, "dp", bit)) for mask, part in got]
            bit //= 2
        for mask, part in got:
            panels = keep(panels, part, section, conv, data ^ mask)

    x_all = checkpoint[0].reshape(micro, rows, channels)
    x_mine = lax.dynamic_index_in_dim(x_all, half, 0, keepdims=False)
    x_other = lax.dynamic_index_in_dim(x_all, 1 - half, 0, keepdims=False)
    x_partner = swap(x_other, "segment", 1)
    k_own = depthwise[0] * tap_mask(genotype[0])[:, None]
    k_partner = swap(k_own, "segment", 1)
    kernels = [jnp.where(is_high, k_partner, k_own), jnp.where(is_high, k_own, k_partner)]
    x_pair = [jnp.where(is_high, x_partner, x_mine), jnp.where(is_high, x_mine, x_partner)]

    saved = [forward(x_pair[s], kernels[s], panels[s, 0], grid) for s in range(2)]
    own_panel = jnp.where(is_high, panels[1, 0], panels[0, 0])
    first_other, _, _, mixed_other = forward(x_other, k_own, own_panel, grid)

    upstream = lax.dynamic_index_in_dim(cotangent, half, 0, keepdims=False).reshape(rows, channels)
    blank = jnp.zeros((rows, channels), jnp.bfloat16)
    state = (blank,) * 8

    for turn in range(pairs):

        def work(upstream, state):
            in_high, pre_high, mix_high, lin_high = backward(
                upstream, x_pair[1], saved[1][2], kernels[1], panels[1, 0], panels[1, 1], grid
            )
            in_low, pre_low, mix_low, lin_low = backward(
                in_high, x_pair[0], saved[0][2], kernels[0], panels[0, 0], panels[0, 1], grid
            )
            return (in_high, pre_high, mix_high, lin_high, in_low, pre_low, mix_low, lin_low)

        def rest(upstream, state):
            return state

        state = lax.cond(pair == pairs - 1 - turn, work, rest, upstream, state)
        if turn < pairs - 1:
            source = pairs - 1 - turn
            arrived = lax.ppermute(
                state[4], "segment", [(2 * source + h, 2 * source - 2 + h) for h in range(2)]
            )
            upstream = jnp.where(pair == source - 1, arrived, upstream)

    in_high, pre_high, mix_high, lin_high, in_low, pre_low, mix_low, lin_low = state
    up_high, up_low = upstream, in_high
    up_mine = jnp.where(is_high, up_high, up_low)
    up_other = swap(jnp.where(is_high, up_low, up_high), "segment", 1)
    pre_mine = jnp.where(is_high, pre_high, pre_low)
    pre_other = swap(jnp.where(is_high, pre_low, pre_high), "segment", 1)
    in_mine = jnp.where(is_high, in_high, in_low)
    in_other = swap(jnp.where(is_high, in_low, in_high), "segment", 1)
    grad_input = jnp.where(is_high, jnp.stack([in_other, in_mine]), jnp.stack([in_mine, in_other]))
    first_mine = jnp.where(is_high, saved[1][0], saved[0][0])
    mixed_mine = jnp.where(is_high, saved[1][3], saved[0][3])

    def scattered(partial):
        blocks = partial.reshape(dp, share, channels).astype(jnp.bfloat16)
        bit = 1
        shape = [2] * (dp.bit_length() - 1)
        blocks = blocks.reshape(shape + [share, channels])
        axis = len(shape) - 1
        while bit < dp:
            mine = (data // bit) % 2
            stay = lax.dynamic_index_in_dim(blocks, mine, axis, keepdims=False)
            leave = lax.dynamic_index_in_dim(blocks, 1 - mine, axis, keepdims=False)
            came = swap(leave, "dp", bit)
            total = stay.astype(jnp.float32) + came.astype(jnp.float32)
            bit *= 2
            axis -= 1
            blocks = total if bit >= dp else total.astype(jnp.bfloat16)
        return blocks * mean_scale

    grad_second = scattered(inner_rows(mixed_mine, up_mine) + inner_rows(mixed_other, up_other))
    grad_first = scattered(inner_rows(first_mine, pre_mine) + inner_rows(first_other, pre_other))
    grad_point = jnp.stack([grad_first, grad_second], 1)

    depth = []
    for s, mix, lin in ((0, mix_low, lin_low), (1, mix_high, lin_high)):
        act = jnp.maximum(x_pair[s], 0).reshape(grid)
        depth.append(
            jnp.stack(
                [
                    kernel_grad(act, lin.reshape(grid)),
                    kernel_grad(saved[s][1].reshape(grid), mix.reshape(grid)),
                ]
            ).astype(jnp.bfloat16)
        )
    depth_mine = jnp.where(is_high, depth[1], depth[0]).astype(jnp.float32)
    came = swap(jnp.where(is_high, depth[0], depth[1]), "segment", 1)
    total = depth_mine + came.astype(jnp.float32)
    bit = 1
    while bit < dp:
        sent = total.astype(jnp.bfloat16)
        total = sent.astype(jnp.float32) + swap(sent, "dp", bit).astype(jnp.float32)
        bit *= 2
    grad_depth = total * tap_mask(genotype[0])[:, None] * mean_scale

    return (
        grad_input.reshape(checkpoint.shape),
        grad_point[None],
        grad_depth[None],
    )


def solution(mesh):
    placed = (
        P("segment", None, "dp", None, None, None),
        P(None, "dp", None, None, None),
        P("segment", None, None, None),
        P("segment", "dp", None, None),
        P("segment"),
    )
    return jax.shard_map(
        body,
        mesh=mesh,
        in_specs=placed,
        out_specs=(
            P("segment", None, "dp", None, None, None),
            P("segment", "dp", None, None),
            P("segment", None, None, None),
        ),
        check_vma=False,
    )
```

```python
import functools
import jax
import jax.numpy as jnp
from jax import lax
from jax.sharding import PartitionSpec as P
from jax.experimental import pallas as pl
from jax.experimental.pallas import tpu as pltpu

LANES = 128
UNROLL = 16
KEPT = (
    [(r, c) for r in (-1, 0, 1) for c in (-1, 0, 1)],
    [(r, c) for r in (-2, -1, 0, 1, 2) for c in (-2, -1, 0, 1, 2)],
    [(r, c) for r in (-2, 0, 2) for c in (-2, 0, 2)],
)


def moved(value, step):
    if step == 0:
        return value
    side = value.shape[0]
    place = lax.broadcasted_iota(jnp.int32, value.shape, 0) + step
    return jnp.where((place >= 0) & (place < side), pltpu.roll(value, (-step) % side, 0), 0.0)


def conv(source, taps, kept, emit):
    side = source.shape[1]
    cols = sorted({c for _, c in kept})
    lines = sorted({r for r, _ in kept})

    def lane(chunk, carry):
        lanes = pl.ds(pl.multiple_of(chunk * LANES, LANES), LANES)
        weight = {(r, c): taps(5 * (r + 2) + c + 2, lanes) for r, c in kept}

        def row(p, carry):
            near = {r: source[p + r + 2, :, lanes] for r in lines}
            total = None
            for c in cols:
                column = None
                for r in lines:
                    term = weight[r, c] * near[r]
                    column = term if column is None else column + term
                column = moved(column, c)
                total = column if total is None else total + column
            emit(pl.ds(pl.multiple_of(p * side, side), side), lanes, total)
            return carry

        lax.fori_loop(0, side, row, 0, unroll=UNROLL)
        return carry

    lax.fori_loop(0, source.shape[2] // LANES, lane, 0)


def clear_edges(source):
    side = source.shape[1]
    zero = jnp.zeros((2,) + source.shape[1:], jnp.float32)
    source[:2] = zero
    source[side + 2 :] = zero


def backward_kernel(scalars, up, x, slope, k, *refs, side, parts):
    second = refs[:parts]
    first = refs[parts : 2 * parts]
    grad_in, pre, mix, lin, source = refs[2 * parts :]
    width = second[0].shape[0]
    clear_edges(source)

    def run(kept):
        for stage in range(2):
            left, panel, kept_flat = (up, second, mix) if stage == 0 else (pre, first, lin)
            for part in range(parts):
                flat = lax.dot_general(
                    left[...], panel[part][...], (((1,), (1,)), ((), ())), preferred_element_type=jnp.float32
                )
                wide = pl.ds(pl.multiple_of((scalars[0] ^ part) * width, LANES), width)
                kept_flat[:, wide] = flat.astype(jnp.bfloat16)
                source[2 : side + 2, :, wide] = flat.reshape(side, side, width)

            def emit(rows, lanes, total):
                if stage == 0:
                    pre[rows, lanes] = (total * slope[rows, lanes].astype(jnp.float32)).astype(jnp.bfloat16)
                else:
                    gated = jnp.where(x[rows, lanes].astype(jnp.float32) > 0, total, 0.0)
                    grad_in[rows, lanes] = (up[rows, lanes].astype(jnp.float32) + gated).astype(jnp.bfloat16)

            conv(source, lambda tap, lanes: k[1 - stage, tap, lanes][None], kept, emit)

    for kind in range(3):
        pl.when(scalars[1] == kind)(functools.partial(run, KEPT[kind]))


def backward(scalars, up, x, slope, k, second, first, side):
    parts = len(second)
    rows, channels = up.shape
    out = jax.ShapeDtypeStruct((rows, channels), jnp.bfloat16)
    vmem = pl.BlockSpec(memory_space=pltpu.VMEM)
    return pl.pallas_call(
        functools.partial(backward_kernel, side=side, parts=parts),
        in_specs=[pl.BlockSpec(memory_space=pltpu.SMEM)] + [vmem] * (4 + 2 * parts),
        out_specs=[vmem] * 4,
        out_shape=[out] * 4,
        scratch_shapes=[pltpu.VMEM((side + 4, side, channels), jnp.float32)],
        compiler_params=pltpu.CompilerParams(vmem_limit_bytes=40 * 2**20),
        cost_estimate=pl.CostEstimate(flops=4 * rows * channels * channels, bytes_accessed=10 * 2**20, transcendentals=0),
    )(scalars, up, x, slope, k, *second, *first)


def forward_kernel(scalars, x, k, *refs, side, parts):
    first = refs[:parts]
    start, hidden, slope, mixed, source = refs[parts:]
    width = first[0].shape[0]
    clear_edges(source)

    def run(kept):
        for stage in range(2):
            for part in range(parts):
                wide = pl.ds(part * width, width)
                if stage == 0:
                    flat = jnp.maximum(x[:, wide].astype(jnp.float32), 0.0)
                else:
                    flat = None
                    for inner in range(parts):
                        below = pl.ds(pl.multiple_of((scalars[0] ^ inner) * width, LANES), width)
                        term = jnp.dot(
                            start[:, below], first[inner][:, wide], preferred_element_type=jnp.float32
                        )
                        flat = term if flat is None else flat + term
                    sigma = jax.nn.sigmoid(flat)
                    rounded = (flat * sigma).astype(jnp.bfloat16)
                    hidden[:, wide] = rounded
                    slope[:, wide] = (sigma * (1.0 + flat * (1.0 - sigma))).astype(jnp.bfloat16)
                    flat = rounded.astype(jnp.float32)
                source[2 : side + 2, :, wide] = flat.reshape(side, side, width)
            out = start if stage == 0 else mixed

            def emit(rows, lanes, total):
                out[rows, lanes] = total.astype(jnp.bfloat16)

            conv(source, lambda tap, lanes: k[stage, tap, lanes][None], kept, emit)

    for kind in range(3):
        pl.when(scalars[1] == kind)(functools.partial(run, KEPT[kind]))


def forward(scalars, x, k, first, side):
    parts = len(first)
    rows, channels = x.shape
    out = jax.ShapeDtypeStruct((rows, channels), jnp.bfloat16)
    vmem = pl.BlockSpec(memory_space=pltpu.VMEM)
    return pl.pallas_call(
        functools.partial(forward_kernel, side=side, parts=parts),
        in_specs=[pl.BlockSpec(memory_space=pltpu.SMEM)] + [vmem] * (2 + parts),
        out_specs=[vmem] * 4,
        out_shape=[out] * 4,
        scratch_shapes=[pltpu.VMEM((side + 4, side, channels), jnp.float32)],
        compiler_params=pltpu.CompilerParams(vmem_limit_bytes=32 * 2**20),
        cost_estimate=pl.CostEstimate(
            flops=2 * rows * channels * channels, bytes_accessed=5 * 2**20, transcendentals=rows * channels
        ),
    )(scalars, x, k, *first)


def taps_kernel(scalars, x, lin, hidden, mix, out, source, *, side):
    channels = x.shape[1]
    clear_edges(source)
    out[...] = jnp.zeros_like(out)

    def run(kept):
        cols = sorted({c for _, c in kept})
        lines = sorted({r for r, _ in kept})
        for which, (value, grad) in enumerate(((x, lin), (hidden, mix))):

            def lane(chunk, carry):
                lanes = pl.ds(pl.multiple_of(chunk * LANES, LANES), LANES)
                flat = value[:, lanes].astype(jnp.float32)
                if which == 0:
                    flat = jnp.maximum(flat, 0.0)
                source[2 : side + 2] = flat.reshape(side, side, LANES)

                def row(p, sums):
                    rows = pl.ds(pl.multiple_of(p * side, side), side)
                    here = grad[rows, lanes].astype(jnp.float32)
                    shifted = {c: moved(here, -c) for c in cols}
                    near = {r: source[p + r + 2] for r in lines}
                    new = []
                    for old, (r, c) in zip(sums, kept):
                        term = near[r] * shifted[c]
                        new.append(old + (term[: side // 2] + term[side // 2 :]))
                    return tuple(new)

                blank = jnp.zeros((side // 2, LANES), jnp.float32)
                sums = lax.fori_loop(0, side, row, (blank,) * len(kept), unroll=4)
                for total, (r, c) in zip(sums, kept):
                    out[which, 5 * (r + 2) + c + 2, lanes] = jnp.sum(total, axis=0)
                return carry

            lax.fori_loop(0, channels // LANES, lane, 0)

    for kind in range(3):
        pl.when(scalars[1] == kind)(functools.partial(run, KEPT[kind]))


def tap_sums(scalars, x, lin, hidden, mix, side):
    channels = x.shape[1]
    vmem = pl.BlockSpec(memory_space=pltpu.VMEM)
    return pl.pallas_call(
        functools.partial(taps_kernel, side=side),
        in_specs=[pl.BlockSpec(memory_space=pltpu.SMEM)] + [vmem] * 4,
        out_specs=vmem,
        out_shape=jax.ShapeDtypeStruct((2, 25, channels), jnp.float32),
        scratch_shapes=[pltpu.VMEM((side + 4, side, LANES), jnp.float32)],
        compiler_params=pltpu.CompilerParams(vmem_limit_bytes=24 * 2**20),
        cost_estimate=pl.CostEstimate(flops=10**8, bytes_accessed=3 * 2**20, transcendentals=0),
    )(scalars, x, lin, hidden, mix)


def swap(value, axis, bit):
    count = lax.axis_size(axis)
    return lax.ppermute(value, axis, [(source, source ^ bit) for source in range(count)])


def inner_rows(left, right):
    return lax.dot_general(
        left, right, (((0,), (0,)), ((), ())), preferred_element_type=jnp.float32
    )


def gathered(piece, data, dp, width):
    share, channels = piece.shape
    got = [(0, piece)]
    bit = dp // 2
    while bit >= 1:
        got = got + [(mask ^ bit, swap(part, "dp", bit)) for mask, part in got]
        bit //= 2
    got = [part for _, part in sorted(got, key=lambda pair: pair[0])]
    if share == width:
        return got, data
    panel = jnp.zeros((channels, channels), piece.dtype)
    for mask, part in enumerate(got):
        panel = lax.dynamic_update_slice(panel, part, ((data ^ mask) * share, 0))
    return [panel[at : at + width] for at in range(0, channels, width)], jnp.zeros_like(data)


def body(checkpoint, cotangent, depthwise, pointwise, genotype):
    micro, images, side = checkpoint.shape[1:4]
    channels = checkpoint.shape[5]
    rows = images * side * side
    dp = lax.axis_size("dp")
    sections = lax.axis_size("segment")
    pairs = sections // 2
    segment = lax.axis_index("segment")
    data = lax.axis_index("dp")
    half = segment % 2
    pair = segment // 2
    is_high = half == 1
    share = channels // dp
    width = 256
    mean_scale = 1.0 / (micro * images * dp)

    x_all = checkpoint[0].reshape(micro, rows, channels)
    x_own = lax.dynamic_index_in_dim(x_all, half, 0, keepdims=False)
    x_other = lax.dynamic_index_in_dim(x_all, 1 - half, 0, keepdims=False)
    x_partner = swap(x_other, "segment", 1)
    kind = genotype[0]
    kind_partner = swap(genotype, "segment", 1)[0]
    k_own = depthwise[0]
    k_partner = swap(k_own, "segment", 1)

    own = jnp.swapaxes(pointwise[0], 0, 1)
    partner = [swap(own[conv], "segment", 1) for conv in range(2)]
    own_blocks = [gathered(own[conv], data, dp, width) for conv in range(2)]
    partner_blocks = [gathered(partner[conv], data, dp, width) for conv in range(2)]
    turned = own_blocks[0][1]
    w_own = [blocks for blocks, _ in own_blocks]
    w_partner = [blocks for blocks, _ in partner_blocks]
    scalars_own = jnp.stack([turned, kind]).astype(jnp.int32)
    scalars_partner = jnp.stack([turned, kind_partner]).astype(jnp.int32)

    first_own, hidden_own, slope_own, mixed_own = forward(scalars_own, x_own, k_own, w_own[0], side)
    _, hidden_partner, slope_partner, _ = forward(scalars_partner, x_partner, k_partner, w_partner[0], side)
    first_other, _, _, mixed_other = forward(scalars_own, x_other, k_own, w_own[0], side)

    upstream = lax.dynamic_index_in_dim(cotangent, half, 0, keepdims=False).reshape(rows, channels)
    blank = jnp.zeros((rows, channels), jnp.bfloat16)
    state = (blank,) * 8
    back_own = k_own[:, ::-1]
    back_partner = k_partner[:, ::-1]

    def through_own(upstream):
        return backward(
            scalars_own, upstream, x_own, slope_own, back_own, w_own[1], w_own[0], side
        )

    def through_partner(upstream):
        return backward(
            scalars_partner, upstream, x_partner, slope_partner, back_partner, w_partner[1], w_partner[0], side
        )

    def rest(upstream, state):
        return state

    def own_first(upstream, state):
        mine = through_own(upstream)
        return tuple(mine) + tuple(through_partner(mine[0]))

    def own_second(upstream, state):
        theirs = through_partner(upstream)
        return tuple(through_own(theirs[0])) + tuple(theirs)

    for turn in range(pairs):
        branch = jnp.where(pair == pairs - 1 - turn, 1 + half, 0)
        state = lax.switch(branch, (rest, own_second, own_first), upstream, state)
        if turn < pairs - 1:
            source = pairs - 1 - turn
            arrived = lax.ppermute(
                jnp.where(is_high, state[4], state[0]),
                "segment",
                [(2 * source + h, 2 * source - 2 + h) for h in range(2)],
            )
            upstream = jnp.where(pair == source - 1, arrived, upstream)

    in_own, pre_own, mix_own, lin_own, in_partner, pre_partner, mix_partner, lin_partner = state
    up_own = jnp.where(is_high, upstream, in_partner)
    up_partner = jnp.where(is_high, in_own, upstream)
    up_other = swap(up_partner, "segment", 1)
    pre_other = swap(pre_partner, "segment", 1)
    in_other = swap(in_partner, "segment", 1)
    grad_input = jnp.where(is_high, jnp.stack([in_other, in_own]), jnp.stack([in_own, in_other]))

    def scattered(partial):
        blocks = partial.astype(jnp.bfloat16).reshape([2] * (dp.bit_length() - 1) + [share, channels])
        axis = dp.bit_length() - 2
        bit = 1
        while bit < dp:
            mine = (data // bit) % 2
            stay = lax.dynamic_index_in_dim(blocks, mine, axis, keepdims=False)
            leave = lax.dynamic_index_in_dim(blocks, 1 - mine, axis, keepdims=False)
            came = swap(leave, "dp", bit)
            total = stay.astype(jnp.float32) + came.astype(jnp.float32)
            bit *= 2
            axis -= 1
            blocks = total if bit >= dp else total.astype(jnp.bfloat16)
        return blocks * mean_scale

    grad_second = scattered(inner_rows(mixed_own, up_own) + inner_rows(mixed_other, up_other))
    grad_first = scattered(inner_rows(first_own, pre_own) + inner_rows(first_other, pre_other))
    grad_point = jnp.stack([grad_first, grad_second], 1)

    sums_own = tap_sums(scalars_own, x_own, lin_own, hidden_own, mix_own, side)
    sums_partner = tap_sums(scalars_partner, x_partner, lin_partner, hidden_partner, mix_partner, side)
    total = sums_own + swap(sums_partner.astype(jnp.bfloat16), "segment", 1).astype(jnp.float32)
    bit = 1
    while bit < dp:
        sent = total.astype(jnp.bfloat16)
        total = sent.astype(jnp.float32) + swap(sent, "dp", bit).astype(jnp.float32)
        bit *= 2
    grad_depth = total * mean_scale

    return (
        grad_input.reshape(checkpoint.shape),
        grad_point[None],
        grad_depth[None],
    )


def solution(mesh):
    placed = (
        P("segment", None, "dp", None, None, None),
        P(None, "dp", None, None, None),
        P("segment", None, None, None),
        P("segment", "dp", None, None),
        P("segment"),
    )
    return jax.shard_map(
        body,
        mesh=mesh,
        in_specs=placed,
        out_specs=(
            P("segment", None, "dp", None, None, None),
            P("segment", "dp", None, None),
            P("segment", None, None, None),
        ),
        check_vma=False,
    )
```

```python
import functools

import jax
import jax.numpy as jnp
from jax import lax
from jax.experimental import pallas as pl
from jax.experimental.pallas import tpu as pltpu
from jax.sharding import PartitionSpec as P

LANES = 128
TAPS = 25
KEPT = (
    [(r, c) for r in (-1, 0, 1) for c in (-1, 0, 1)],
    [(r, c) for r in (-2, -1, 0, 1, 2) for c in (-2, -1, 0, 1, 2)],
    [(r, c) for r in (-2, 0, 2) for c in (-2, 0, 2)],
)
MIB = 2**20


def moved(value, step):
    if step == 0:
        return value
    side = value.shape[0]
    place = lax.broadcasted_iota(jnp.int32, value.shape, 0) + step
    return jnp.where((place >= 0) & (place < side), pltpu.roll(value, (-step) % side, 0), 0.0)


def conv(source, taps, kind, emit):
    side = source.shape[1]

    def run(kept):
        cols = sorted({c for _, c in kept})
        lines = sorted({r for r, _ in kept})

        def lane(chunk, carry):
            lanes = pl.ds(pl.multiple_of(chunk * LANES, LANES), LANES)
            weight = {(r, c): taps(5 * (r + 2) + c + 2, lanes) for r, c in kept}

            def row(p, carry):
                near = {r: source[p + r + 2, :, lanes] for r in lines}
                total = None
                for c in cols:
                    column = None
                    for r in lines:
                        term = weight[r, c] * near[r]
                        column = term if column is None else column + term
                    column = moved(column, c)
                    total = column if total is None else total + column
                emit(pl.ds(pl.multiple_of(p * side, side), side), lanes, total)
                return carry

            lax.fori_loop(0, side, row, 0, unroll=16)
            return carry

        lax.fori_loop(0, source.shape[2] // LANES, lane, 0)

    for which in range(3):
        pl.when(kind == which)(functools.partial(run, KEPT[which]))


def clear_edges(source):
    side = source.shape[1]
    zero = jnp.zeros((2,) + source.shape[1:], jnp.float32)
    source[:2] = zero
    source[side + 2 :] = zero


def chain_kernel(scalars, *refs, visits, parts, aliased, side):
    up_in = refs[0]
    xs, slopes, ks = refs[1:3], refs[3:5], refs[5:7]
    blocks = (refs[7 : 7 + parts], refs[7 + parts : 7 + 2 * parts])
    at = 7 + 2 * parts + aliased
    up_out, in_out, pre_out, mix_out, lin_out, leave = (
        refs[at : at + 2],
        refs[at + 2 : at + 4],
        refs[at + 4 : at + 6],
        refs[at + 6 : at + 8],
        refs[at + 8 : at + 10],
        refs[at + 10],
    )
    panels, x_at, slope_at, k_at, up_at, in_at, pre_at, mix_at, lin_at, source, came, went = refs[at + 11 :]
    width = panels.shape[3]

    def go(order):
        clear_edges(source)
        pending = {}

        def fetch(name, src, dst):
            copy = pltpu.make_async_copy(src, dst, came.at[len(pending)])
            copy.start()
            pending[name] = copy

        fetch("up", up_in, up_at)
        for visit in visits:
            slot = order[visit]
            for part in range(parts):
                fetch(("w", visit, 1, part), blocks[slot][part].at[1], panels.at[visit, 1, part])
            fetch(("k", visit), ks[slot], k_at.at[visit])
            fetch(("slope", visit), slopes[slot], slope_at.at[visit])
            for part in range(parts):
                fetch(("w", visit, 0, part), blocks[slot][part].at[0], panels.at[visit, 0, part])
            fetch(("x", visit), xs[slot], x_at.at[visit])
        leaving = []

        def send(src, dst):
            copy = pltpu.make_async_copy(src, dst, went.at[len(leaving)])
            copy.start()
            leaving.append(copy)

        pending["up"].wait()
        for visit in visits:
            slot = order[visit]
            kind = scalars[1 + slot]
            up = up_at if visit == visits[0] else in_at.at[visits[0]]
            send(up, up_out[slot])
            pre, mix, lin, grad_in = pre_at.at[visit], mix_at.at[visit], lin_at.at[visit], in_at.at[visit]
            k, slope, x = k_at.at[visit], slope_at.at[visit], x_at.at[visit]
            for stage in range(2):
                left, flat_at = (up, mix) if stage == 0 else (pre, lin)
                for part in range(parts):
                    pending["w", visit, 1 - stage, part].wait()
                    flat = lax.dot_general(
                        left[...],
                        panels[visit, 1 - stage, part],
                        (((1,), (1,)), ((), ())),
                        preferred_element_type=jnp.float32,
                    )
                    wide = pl.ds(pl.multiple_of((scalars[0] ^ part) * width, LANES), width)
                    flat_at[:, wide] = flat.astype(jnp.bfloat16)
                    source[2 : side + 2, :, wide] = flat.reshape(side, side, width)
                send(flat_at, (mix_out if stage == 0 else lin_out)[slot])
                if stage == 0:
                    pending["k", visit].wait()
                    pending["slope", visit].wait()
                else:
                    pending["x", visit].wait()

                def emit(rows, lanes, total):
                    if stage == 0:
                        pre[rows, lanes] = (total * slope[rows, lanes].astype(jnp.float32)).astype(jnp.bfloat16)
                    else:
                        gated = jnp.where(x[rows, lanes].astype(jnp.float32) > 0, total, 0.0)
                        grad_in[rows, lanes] = (up[rows, lanes].astype(jnp.float32) + gated).astype(jnp.bfloat16)

                conv(source, lambda tap, lanes: k[(1 - stage) * TAPS + TAPS - 1 - tap, lanes][None], kind, emit)
                send(pre if stage == 0 else grad_in, (pre_out if stage == 0 else in_out)[slot])
            if visit == visits[-1]:
                send(grad_in, leave)
        for copy in leaving:
            copy.wait()

    active = scalars[4] == 1
    pl.when(active & (scalars[3] == 1))(functools.partial(go, (0, 1)))
    pl.when(active & (scalars[3] == 0))(functools.partial(go, (1, 0)))


def chain(scalars, up, xs, slopes, ks, blocks, state, visits, side):
    parts = len(blocks[0])
    rows, channels = up.shape
    taps = ks[0].shape[0]
    flat = jax.ShapeDtypeStruct((rows, channels), jnp.bfloat16)
    anywhere = pl.BlockSpec(memory_space=pl.ANY)
    inputs = [up, *xs, *slopes, *ks, *blocks[0], *blocks[1], *state]
    held = pltpu.VMEM((2, rows, channels), jnp.bfloat16)
    first_state = 1 + len(inputs) - len(state)
    outs = pl.pallas_call(
        functools.partial(chain_kernel, visits=visits, parts=parts, aliased=len(state), side=side),
        in_specs=[pl.BlockSpec(memory_space=pltpu.SMEM)] + [anywhere] * len(inputs),
        out_specs=[anywhere] * 11,
        out_shape=[flat] * 11,
        input_output_aliases={first_state + i: i for i in range(len(state))},
        scratch_shapes=[
            pltpu.VMEM((2, 2, parts, channels // parts, channels), jnp.bfloat16),
            held,
            held,
            pltpu.VMEM((2, taps, channels), jnp.float32),
            pltpu.VMEM((rows, channels), jnp.bfloat16),
            held,
            held,
            held,
            held,
            pltpu.VMEM((side + 4, side, channels), jnp.float32),
            pltpu.SemaphoreType.DMA((1 + 2 * (3 + 2 * parts),)),
            pltpu.SemaphoreType.DMA((11,)),
        ],
        compiler_params=pltpu.CompilerParams(vmem_limit_bytes=28 * MIB, has_side_effects=False),
        cost_estimate=pl.CostEstimate(
            flops=4 * len(visits) * rows * channels * channels, bytes_accessed=12 * MIB, transcendentals=0
        ),
    )(scalars, *inputs)
    return tuple(outs[:10]), outs[10]


def start_kernel(scalars, x, k, start, source, *, slot, side):
    clear_edges(source)
    source[2 : side + 2] = jnp.maximum(x[...].astype(jnp.float32), 0.0).reshape(side, side, x.shape[1])

    def emit(rows, lanes, total):
        start[rows, lanes] = total.astype(jnp.bfloat16)

    conv(source, lambda tap, lanes: k[tap, lanes][None], scalars[1 + slot], emit)


def rest_kernel(scalars, start, k, *refs, slot, side, parts, mixes):
    blocks = refs[:parts]
    outs = refs[parts:]
    hidden, slope = outs[:2]
    width = blocks[0].shape[1]
    if mixes:
        mixed, source = outs[2:]
        clear_edges(source)
    for part in range(parts):
        wide = pl.ds(part * width, width)
        flat = None
        for inner in range(parts):
            below = pl.ds(pl.multiple_of((scalars[0] ^ inner) * width, LANES), width)
            term = jnp.dot(start[:, below], blocks[inner][0, :, wide], preferred_element_type=jnp.float32)
            flat = term if flat is None else flat + term
        sigma = jax.nn.sigmoid(flat)
        rounded = (flat * sigma).astype(jnp.bfloat16)
        hidden[:, wide] = rounded
        slope[:, wide] = (sigma * (1.0 + flat * (1.0 - sigma))).astype(jnp.bfloat16)
        if mixes:
            source[2 : side + 2, :, wide] = rounded.astype(jnp.float32).reshape(side, side, width)
    if mixes:

        def emit(rows, lanes, total):
            mixed[rows, lanes] = total.astype(jnp.bfloat16)

        conv(source, lambda tap, lanes: k[TAPS + tap, lanes][None], scalars[1 + slot], emit)


SMEM = pl.BlockSpec(memory_space=pltpu.SMEM)
VMEM = pl.BlockSpec(memory_space=pltpu.VMEM)


def forward_start(scalars, x, k, slot, side):
    rows, channels = x.shape
    return pl.pallas_call(
        functools.partial(start_kernel, slot=slot, side=side),
        in_specs=[SMEM, VMEM, VMEM],
        out_specs=VMEM,
        out_shape=jax.ShapeDtypeStruct((rows, channels), jnp.bfloat16),
        scratch_shapes=[pltpu.VMEM((side + 4, side, channels), jnp.float32)],
        compiler_params=pltpu.CompilerParams(vmem_limit_bytes=16 * MIB),
        cost_estimate=pl.CostEstimate(flops=10**9, bytes_accessed=MIB, transcendentals=0),
    )(scalars, x, k)


def forward_rest(scalars, start, k, blocks, slot, side, mixes):
    parts = len(blocks)
    rows, channels = start.shape
    outs = 3 if mixes else 2
    return pl.pallas_call(
        functools.partial(rest_kernel, slot=slot, side=side, parts=parts, mixes=mixes),
        in_specs=[SMEM, VMEM, VMEM] + [VMEM] * parts,
        out_specs=[VMEM] * outs,
        out_shape=[jax.ShapeDtypeStruct((rows, channels), jnp.bfloat16)] * outs,
        scratch_shapes=[pltpu.VMEM((side + 4, side, channels), jnp.float32)] if mixes else [],
        compiler_params=pltpu.CompilerParams(vmem_limit_bytes=24 * MIB),
        cost_estimate=pl.CostEstimate(
            flops=2 * rows * channels * channels, bytes_accessed=6 * MIB, transcendentals=rows * channels
        ),
    )(scalars, start, k, *blocks)


def taps_kernel(scalars, x, lin, hidden, mix, out, source, *, slot, side):
    channels = x.shape[1]
    clear_edges(source)
    out[...] = jnp.zeros_like(out)

    def run(kept):
        cols = sorted({c for _, c in kept})
        lines = sorted({r for r, _ in kept})
        for which, (value, grad) in enumerate(((x, lin), (hidden, mix))):

            def lane(chunk, carry):
                lanes = pl.ds(pl.multiple_of(chunk * LANES, LANES), LANES)
                flat = value[:, lanes].astype(jnp.float32)
                if which == 0:
                    flat = jnp.maximum(flat, 0.0)
                source[2 : side + 2] = flat.reshape(side, side, LANES)

                def row(p, sums):
                    rows = pl.ds(pl.multiple_of(p * side, side), side)
                    here = grad[rows, lanes].astype(jnp.float32)
                    shifted = {c: moved(here, -c) for c in cols}
                    near = {r: source[p + r + 2] for r in lines}
                    new = []
                    for old, (r, c) in zip(sums, kept):
                        term = near[r] * shifted[c]
                        new.append(old + (term[: side // 2] + term[side // 2 :]))
                    return tuple(new)

                blank = jnp.zeros((side // 2, LANES), jnp.float32)
                sums = lax.fori_loop(0, side, row, (blank,) * len(kept), unroll=4)
                for total, (r, c) in zip(sums, kept):
                    out[which, 5 * (r + 2) + c + 2, lanes] = jnp.sum(total, axis=0)
                return carry

            lax.fori_loop(0, channels // LANES, lane, 0)

    for kind in range(3):
        pl.when(scalars[1 + slot] == kind)(functools.partial(run, KEPT[kind]))


def tap_sums(scalars, x, lin, hidden, mix, slot, side):
    channels = x.shape[1]
    return pl.pallas_call(
        functools.partial(taps_kernel, slot=slot, side=side),
        in_specs=[SMEM] + [VMEM] * 4,
        out_specs=VMEM,
        out_shape=jax.ShapeDtypeStruct((2, TAPS, channels), jnp.float32),
        scratch_shapes=[pltpu.VMEM((side + 4, side, LANES), jnp.float32)],
        compiler_params=pltpu.CompilerParams(vmem_limit_bytes=16 * MIB),
        cost_estimate=pl.CostEstimate(flops=10**9, bytes_accessed=3 * MIB, transcendentals=0),
    )(scalars, x, lin, hidden, mix)


def swap(value, axis, bit):
    count = lax.axis_size(axis)
    return lax.ppermute(value, axis, [(source, source ^ bit) for source in range(count)])


def inner_rows(left, right):
    return lax.dot_general(
        left, right, (((0,), (0,)), ((), ())), preferred_element_type=jnp.float32
    )


def gathered(piece, data, dp, width):
    share, channels = piece.shape[1:]
    got = [(0, piece)]
    bit = dp // 2
    while bit >= 1:
        got = got + [(mask ^ bit, swap(part, "dp", bit)) for mask, part in got]
        bit //= 2
    got = [part for _, part in sorted(got, key=lambda pair: pair[0])]
    if share == width:
        return got, data
    panel = jnp.zeros((2, channels, channels), piece.dtype)
    for mask, part in enumerate(got):
        panel = lax.dynamic_update_slice(panel, part, (0, (data ^ mask) * share, 0))
    return [panel[:, at : at + width] for at in range(0, channels, width)], jnp.zeros_like(data)


def body(checkpoint, cotangent, depthwise, pointwise, genotype):
    micro, images, side = checkpoint.shape[1:4]
    channels = checkpoint.shape[5]
    rows = images * side * side
    dp = lax.axis_size("dp")
    sections = lax.axis_size("segment")
    pairs = sections // 2
    segment = lax.axis_index("segment")
    data = lax.axis_index("dp")
    half = segment % 2
    pair = segment // 2
    is_high = half == 1
    share = channels // dp
    width = 256
    mean_scale = 1.0 / (micro * images * dp)

    own = jnp.swapaxes(pointwise[0], 0, 1)
    partner = swap(own, "segment", 1)
    own_blocks, turned = gathered(own, data, dp, width)
    partner_blocks, _ = gathered(partner, data, dp, width)
    blocks = (own_blocks, partner_blocks)

    x_all = checkpoint[0].reshape(micro, rows, channels)
    x_own = lax.dynamic_index_in_dim(x_all, half, 0, keepdims=False)
    x_other = lax.dynamic_index_in_dim(x_all, 1 - half, 0, keepdims=False)
    x_partner = swap(x_other, "segment", 1)
    kind_row = jnp.full((1, channels), genotype[0].astype(jnp.float32))
    k_own = jnp.concatenate([depthwise[0].reshape(2 * TAPS, channels), kind_row])
    k_partner = swap(k_own, "segment", 1)
    kind_partner = k_partner[2 * TAPS, 0].astype(jnp.int32)

    def scalars_for(active, kind_partner=kind_partner):
        return jnp.stack([turned, genotype[0], kind_partner, half, active]).astype(jnp.int32)

    scalars_own = scalars_for(0, genotype[0])
    scalars = scalars_for(0)

    first_own = forward_start(scalars_own, x_own, k_own, 0, side)
    first_other = forward_start(scalars_own, x_other, k_own, 0, side)
    hidden_own, slope_own, mixed_own = forward_rest(scalars_own, first_own, k_own, own_blocks, 0, side, True)
    _, _, mixed_other = forward_rest(scalars_own, first_other, k_own, own_blocks, 0, side, True)
    first_partner = forward_start(scalars, x_partner, k_partner, 1, side)
    hidden_partner, slope_partner = forward_rest(
        scalars, first_partner, k_partner, partner_blocks, 1, side, False
    )

    upstream = lax.dynamic_index_in_dim(cotangent, half, 0, keepdims=False).reshape(rows, channels)
    xs, slopes, ks = (x_own, x_partner), (slope_own, slope_partner), (k_own, k_partner)
    state = ()
    for turn in range(pairs):
        source = pairs - 1 - turn
        now = scalars_for((pair == source).astype(jnp.int32))
        if turn < pairs - 1:
            state, leaving = chain(now, upstream, xs, slopes, ks, blocks, state, (0, 1), side)
            upstream = lax.ppermute(
                leaving, "segment", [(2 * source + h, 2 * source - 2 + h) for h in range(2)]
            )
            if turn == 0:
                state, (first_other, mixed_other) = lax.optimization_barrier(
                    (state, (first_other, mixed_other))
                )
        else:
            state, leaving = chain(now, upstream, xs, slopes, ks, blocks, state, (0,), side)
            fresh = is_high & (pair == source)
            up_other = swap(jnp.where(fresh, leaving, state[1]), "segment", 1)
            state, _ = chain(now, leaving, xs, slopes, ks, blocks, state, (1,), side)

    up_own, _, in_own, in_partner, pre_own, pre_partner, mix_own, mix_partner, lin_own, lin_partner = state
    pre_other = swap(pre_partner, "segment", 1)
    in_other = swap(in_partner, "segment", 1)
    grad_input = jnp.where(is_high, jnp.stack([in_other, in_own]), jnp.stack([in_own, in_other]))

    def scattered(left_own, left_other, right_own, right_other):
        def product(core):
            def rows_of(left):
                left = left.reshape(rows, dp // 2, 2, share)
                return lax.dynamic_index_in_dim(left, core, 2, keepdims=False).reshape(rows, -1)

            return inner_rows(rows_of(left_own), right_own) + inner_rows(rows_of(left_other), right_other)

        mine = data % 2
        came = swap(product(1 - mine).astype(jnp.bfloat16), "dp", 1)
        total = product(mine) + came.astype(jnp.float32)
        shape = [2] * (dp.bit_length() - 2) + [share, channels]
        total = total.reshape(shape)
        axis = len(shape) - 3
        bit = 2
        while bit < dp:
            mine = (data // bit) % 2
            stay = lax.dynamic_index_in_dim(total, mine, axis, keepdims=False)
            leave = lax.dynamic_index_in_dim(total, 1 - mine, axis, keepdims=False)
            total = stay + swap(leave.astype(jnp.bfloat16), "dp", bit).astype(jnp.float32)
            bit *= 2
            axis -= 1
        return total * mean_scale

    grad_second = scattered(mixed_own, mixed_other, up_own, up_other)
    grad_first = scattered(first_own, first_other, pre_own, pre_other)
    grad_point = jnp.stack([grad_first, grad_second], 1)

    sums_own = tap_sums(scalars, x_own, lin_own, hidden_own, mix_own, 0, side)
    sums_partner = tap_sums(scalars, x_partner, lin_partner, hidden_partner, mix_partner, 1, side)
    total = sums_own + swap(sums_partner.astype(jnp.bfloat16), "segment", 1).astype(jnp.float32)
    bit = 1
    while bit < dp:
        sent = total.astype(jnp.bfloat16)
        total = sent.astype(jnp.float32) + swap(sent, "dp", bit).astype(jnp.float32)
        bit *= 2
    grad_depth = total * mean_scale

    return (
        grad_input.reshape(checkpoint.shape),
        grad_point[None],
        grad_depth[None],
    )


def solution(mesh):
    placed = (
        P("segment", None, "dp", None, None, None),
        P(None, "dp", None, None, None),
        P("segment", None, None, None),
        P("segment", "dp", None, None),
        P("segment"),
    )
    return jax.shard_map(
        body,
        mesh=mesh,
        in_specs=placed,
        out_specs=(
            P("segment", None, "dp", None, None, None),
            P("segment", "dp", None, None),
            P("segment", None, None, None),
        ),
        check_vma=False,
    )
```

```python
import functools

import jax
import jax.numpy as jnp
from jax import lax
from jax.experimental import pallas as pl
from jax.experimental.pallas import tpu as pltpu
from jax.sharding import PartitionSpec as P

LANES = 128
TAPS = 25
KEPT = (
    [(r, c) for r in (-1, 0, 1) for c in (-1, 0, 1)],
    [(r, c) for r in (-2, -1, 0, 1, 2) for c in (-2, -1, 0, 1, 2)],
    [(r, c) for r in (-2, 0, 2) for c in (-2, 0, 2)],
)
MIB = 2**20


def moved(value, step):
    if step == 0:
        return value
    side = value.shape[0]
    place = lax.broadcasted_iota(jnp.int32, value.shape, 0) + step
    return jnp.where((place >= 0) & (place < side), pltpu.roll(value, (-step) % side, 0), 0.0)


def conv(source, taps, kind, emit):
    side = source.shape[1]

    def run(kept):
        cols = sorted({c for _, c in kept})
        lines = sorted({r for r, _ in kept})

        def lane(chunk, carry):
            lanes = pl.ds(pl.multiple_of(chunk * LANES, LANES), LANES)
            weight = {(r, c): taps(5 * (r + 2) + c + 2, lanes) for r, c in kept}

            def row(p, carry):
                near = {r: source[p + r + 2, :, lanes] for r in lines}
                total = None
                for c in cols:
                    column = None
                    for r in lines:
                        term = weight[r, c] * near[r]
                        column = term if column is None else column + term
                    column = moved(column, c)
                    total = column if total is None else total + column
                emit(pl.ds(pl.multiple_of(p * side, side), side), lanes, total)
                return carry

            lax.fori_loop(0, side, row, 0, unroll=16)
            return carry

        lax.fori_loop(0, source.shape[2] // LANES, lane, 0)

    for which in range(3):
        pl.when(kind == which)(functools.partial(run, KEPT[which]))


def clear_edges(source):
    side = source.shape[1]
    zero = jnp.zeros((2,) + source.shape[1:], jnp.float32)
    source[:2] = zero
    source[side + 2 :] = zero


def chain_kernel(scalars, *refs, pair, visits, parts, aliased, side):
    up_in = refs[0]
    xs, slopes, ks = refs[1:3], refs[3:5], refs[5:7]
    blocks = (refs[7 : 7 + parts], refs[7 + parts : 7 + 2 * parts])
    at = 7 + 2 * parts + aliased
    held = 4 if visits[0] else 5
    outs = [refs[at + 2 * i : at + 2 * i + 2] for i in range(held)]
    in_out, pre_out, mix_out, lin_out = outs[:4]
    leave = refs[at + 2 * held]
    panels, factor, k_at, left_at, flat_at, source, came, went = refs[at + 2 * held + 1 :]
    width = panels.shape[1] // parts
    steps = 2 * len(visits)

    def piece(step, part):
        return panels.at[step, pl.ds(part * width, width)], came.at[step * (parts + 1) + part]

    def other(step):
        return factor.at[step], came.at[step * (parts + 1) + parts]

    def taps_of(visit):
        return k_at.at[visit], came.at[steps * (parts + 1) + visit]

    def fetch(order):
        for index, visit in enumerate(visits):
            slot = order[visit]
            for stage in range(2):
                step = 2 * index + stage
                for part in range(parts):
                    place, sem = piece(step, part)
                    pltpu.make_async_copy(blocks[slot][part].at[1 - stage], place, sem).start()
                if stage == 0:
                    place, sem = taps_of(index)
                    pltpu.make_async_copy(ks[slot], place, sem).start()
                place, sem = other(step)
                pltpu.make_async_copy((xs if stage else slopes)[slot], place, sem).start()

    def send(value, outs, slot, sem):
        for which in range(2):
            pl.when(slot == which)(pltpu.make_async_copy(value, outs[which], went.at[sem]).start)

    def wait(place, sem):
        pltpu.make_async_copy(place, place, sem).wait()

    def go():
        first = pltpu.make_async_copy(up_in, left_at.at[0], came.at[steps * (parts + 1) + len(visits)])
        first.start()
        pl.when(scalars[3] == 1)(functools.partial(fetch, (0, 1)))
        pl.when(scalars[3] == 0)(functools.partial(fetch, (1, 0)))
        clear_edges(source)
        first.wait()

        def one(step, carry):
            index = step // 2
            stage = step % 2
            slot = (visits[0] + index) ^ (1 - scalars[3])
            left = left_at.at[step]

            def multiply(part, carry):
                place, sem = piece(step, part)
                wait(place, sem)
                flat = lax.dot_general(
                    left[...], place[...], (((1,), (1,)), ((), ())), preferred_element_type=jnp.float32
                )
                wide = pl.ds(pl.multiple_of((scalars[0] ^ part) * width, LANES), width)
                flat_at[step, :, wide] = flat.astype(jnp.bfloat16)
                source[2 : side + 2, :, wide] = flat.reshape(side, side, width)
                return carry

            lax.fori_loop(0, parts, multiply, 0)

            @pl.when(stage == 0)
            def _():
                wait(*taps_of(index))
                if visits[0] == 0:
                    send(left, outs[4], slot, 3 * step)
                send(flat_at.at[step], mix_out, slot, 3 * step + 1)

            @pl.when(stage == 1)
            def _():
                send(flat_at.at[step], lin_out, slot, 3 * step + 1)

            wait(*other(step))
            result = left_at.at[step + 1]

            def taps(tap, lanes):
                return k_at[index, 1 - stage, TAPS - 1 - tap, lanes][None]

            def emit(rows, lanes, total):
                scale = factor[step, rows, lanes].astype(jnp.float32)
                scale = jnp.where(stage == 0, scale, jnp.where(scale > 0, 1.0, 0.0))
                base = left_at[2 * index, rows, lanes].astype(jnp.float32)
                base = jnp.where(stage == 0, 0.0, base)
                result[rows, lanes] = (base + total * scale).astype(jnp.bfloat16)

            conv(source, taps, scalars[1 + slot], emit)

            @pl.when(stage == 0)
            def _():
                send(result, pre_out, slot, 3 * step + 2)

            @pl.when(stage == 1)
            def _():
                send(result, in_out, slot, 3 * step + 2)
                if len(visits) == 1 and visits[0] == 0:
                    send(result, outs[4], 1 - slot, 3 * step)

            return carry

        lax.fori_loop(0, steps, one, 0)
        last = pltpu.make_async_copy(left_at.at[steps], leave, came.at[0])
        last.start()
        for step in range(steps):
            for which in range(3):
                if which > 0 or (step % 2 == 0 and visits[0] == 0) or visits == (0,):
                    wait(flat_at.at[0], went.at[3 * step + which])
        last.wait()

    pl.when(scalars[4] == pair)(go)


def chain(scalars, up, xs, slopes, ks, blocks, state, pair, visits, side):
    parts = len(blocks[0])
    rows, channels = up.shape
    steps = 2 * len(visits)
    flat = jax.ShapeDtypeStruct((rows, channels), jnp.bfloat16)
    anywhere = pl.BlockSpec(memory_space=pl.ANY)
    inputs = [up, *xs, *slopes, *ks, *blocks[0], *blocks[1], *state]
    first_state = 1 + len(inputs) - len(state)
    count = 8 if visits[0] else 10
    outs = pl.pallas_call(
        functools.partial(chain_kernel, pair=pair, visits=visits, parts=parts, aliased=len(state), side=side),
        in_specs=[pl.BlockSpec(memory_space=pltpu.SMEM)] + [anywhere] * len(inputs),
        out_specs=[anywhere] * (count + 1),
        out_shape=[flat] * (count + 1),
        input_output_aliases={first_state + i: i for i in range(len(state))},
        scratch_shapes=[
            pltpu.VMEM((steps, channels, channels), jnp.bfloat16),
            pltpu.VMEM((steps, rows, channels), jnp.bfloat16),
            pltpu.VMEM((len(visits),) + ks[0].shape, jnp.float32),
            pltpu.VMEM((steps + 1, rows, channels), jnp.bfloat16),
            pltpu.VMEM((steps, rows, channels), jnp.bfloat16),
            pltpu.VMEM((side + 4, side, channels), jnp.float32),
            pltpu.SemaphoreType.DMA((steps * (parts + 1) + len(visits) + 1,)),
            pltpu.SemaphoreType.DMA((3 * steps,)),
        ],
        compiler_params=pltpu.CompilerParams(vmem_limit_bytes=58 * MIB),
        cost_estimate=pl.CostEstimate(flops=10**10, bytes_accessed=12 * MIB, transcendentals=0),
    )(scalars, *inputs)
    return tuple(outs[:count]), outs[count]


def start_kernel(scalars, x, k, start, source, *, slot, side):
    clear_edges(source)
    source[2 : side + 2] = jnp.maximum(x[...].astype(jnp.float32), 0.0).reshape(side, side, x.shape[1])

    def emit(rows, lanes, total):
        start[rows, lanes] = total.astype(jnp.bfloat16)

    conv(source, lambda tap, lanes: k[0, tap, lanes][None], scalars[1 + slot], emit)


def rest_kernel(scalars, start, *refs, slot, side, parts, mixes):
    if mixes:
        k, *refs = refs
    blocks = refs[:parts]
    panel, came = refs[-2:]
    hidden, slope = refs[parts : parts + 2]
    width = blocks[0].shape[1]
    copies = [pltpu.make_async_copy(blocks[part].at[0], panel.at[part], came.at[part]) for part in range(parts)]
    for copy in copies:
        copy.start()
    if mixes:
        mixed, source = refs[parts + 2 : parts + 4]
        clear_edges(source)
    for copy in copies:
        copy.wait()

    def columns(part, carry):
        wide = pl.ds(pl.multiple_of(part * width, LANES), width)
        flat = None
        for inner in range(parts):
            below = pl.ds(pl.multiple_of((scalars[0] ^ inner) * width, LANES), width)
            term = jnp.dot(start[:, below], panel[inner, :, wide], preferred_element_type=jnp.float32)
            flat = term if flat is None else flat + term
        sigma = jax.nn.sigmoid(flat)
        rounded = (flat * sigma).astype(jnp.bfloat16)
        hidden[:, wide] = rounded
        slope[:, wide] = (sigma * (1.0 + flat * (1.0 - sigma))).astype(jnp.bfloat16)
        if mixes:
            source[2 : side + 2, :, wide] = rounded.astype(jnp.float32).reshape(side, side, width)
        return carry

    lax.fori_loop(0, parts, columns, 0)
    if mixes:

        def emit(rows, lanes, total):
            mixed[rows, lanes] = total.astype(jnp.bfloat16)

        conv(source, lambda tap, lanes: k[1, tap, lanes][None], scalars[1 + slot], emit)


SMEM = pl.BlockSpec(memory_space=pltpu.SMEM)
VMEM = pl.BlockSpec(memory_space=pltpu.VMEM)


def forward_start(scalars, x, k, slot, side):
    rows, channels = x.shape
    return pl.pallas_call(
        functools.partial(start_kernel, slot=slot, side=side),
        in_specs=[SMEM, VMEM, VMEM],
        out_specs=VMEM,
        out_shape=jax.ShapeDtypeStruct((rows, channels), jnp.bfloat16),
        scratch_shapes=[pltpu.VMEM((side + 4, side, channels), jnp.float32)],
        compiler_params=pltpu.CompilerParams(vmem_limit_bytes=58 * MIB),
        cost_estimate=pl.CostEstimate(flops=1, bytes_accessed=1, transcendentals=0),
    )(scalars, x, k)


def forward_rest(scalars, start, k, blocks, slot, side, mixes):
    parts = len(blocks)
    rows, channels = start.shape
    outs = 3 if mixes else 2
    return pl.pallas_call(
        functools.partial(rest_kernel, slot=slot, side=side, parts=parts, mixes=mixes),
        in_specs=[SMEM, VMEM] + [VMEM] * mixes + [pl.BlockSpec(memory_space=pl.ANY)] * parts,
        out_specs=[VMEM] * outs,
        out_shape=[jax.ShapeDtypeStruct((rows, channels), jnp.bfloat16)] * outs,
        scratch_shapes=([pltpu.VMEM((side + 4, side, channels), jnp.float32)] if mixes else [])
        + [pltpu.VMEM((parts, channels // parts, channels), jnp.bfloat16), pltpu.SemaphoreType.DMA((parts,))],
        compiler_params=pltpu.CompilerParams(vmem_limit_bytes=58 * MIB),
        cost_estimate=pl.CostEstimate(flops=1, bytes_accessed=1, transcendentals=0),
    )(scalars, start, *([k] if mixes else []), *blocks)


def taps_kernel(scalars, x, lin, hidden, mix, out, source, *, slot, side):
    channels = x.shape[1]
    clear_edges(source)
    out[...] = jnp.zeros_like(out)

    def run(kept):
        cols = sorted({c for _, c in kept})
        lines = sorted({r for r, _ in kept})
        for which, (value, grad) in enumerate(((x, lin), (hidden, mix))):

            def lane(chunk, carry):
                lanes = pl.ds(pl.multiple_of(chunk * LANES, LANES), LANES)
                flat = value[:, lanes].astype(jnp.float32)
                if which == 0:
                    flat = jnp.maximum(flat, 0.0)
                source[2 : side + 2] = flat.reshape(side, side, LANES)

                def row(p, sums):
                    rows = pl.ds(pl.multiple_of(p * side, side), side)
                    here = grad[rows, lanes].astype(jnp.float32)
                    shifted = {c: moved(here, -c) for c in cols}
                    near = {r: source[p + r + 2] for r in lines}
                    new = []
                    for old, (r, c) in zip(sums, kept):
                        term = near[r] * shifted[c]
                        new.append(old + (term[: side // 2] + term[side // 2 :]))
                    return tuple(new)

                blank = jnp.zeros((side // 2, LANES), jnp.float32)
                sums = lax.fori_loop(0, side, row, (blank,) * len(kept), unroll=4)
                for total, (r, c) in zip(sums, kept):
                    out[which, 5 * (r + 2) + c + 2, lanes] = jnp.sum(total, axis=0)
                return carry

            lax.fori_loop(0, channels // LANES, lane, 0)

    for kind in range(3):
        pl.when(scalars[1 + slot] == kind)(functools.partial(run, KEPT[kind]))


def tap_sums(scalars, x, lin, hidden, mix, slot, side):
    channels = x.shape[1]
    return pl.pallas_call(
        functools.partial(taps_kernel, slot=slot, side=side),
        in_specs=[SMEM] + [VMEM] * 4,
        out_specs=VMEM,
        out_shape=jax.ShapeDtypeStruct((2, TAPS, channels), jnp.float32),
        scratch_shapes=[pltpu.VMEM((side + 4, side, LANES), jnp.float32)],
        compiler_params=pltpu.CompilerParams(vmem_limit_bytes=58 * MIB),
        cost_estimate=pl.CostEstimate(flops=1, bytes_accessed=1, transcendentals=0),
    )(scalars, x, lin, hidden, mix)


def joined_kernel(first, first_came, second, second_came, out, *, scale):
    out[:, 0, :] = (first[...] + first_came[...].astype(jnp.float32)) * scale
    out[:, 1, :] = (second[...] + second_came[...].astype(jnp.float32)) * scale


def joined(first, first_came, second, second_came, scale):
    share, channels = first.shape
    return pl.pallas_call(
        functools.partial(joined_kernel, scale=scale),
        in_specs=[VMEM] * 4,
        out_specs=VMEM,
        out_shape=jax.ShapeDtypeStruct((share, 2, channels), jnp.float32),
        compiler_params=pltpu.CompilerParams(vmem_limit_bytes=24 * MIB),
        cost_estimate=pl.CostEstimate(flops=1, bytes_accessed=1, transcendentals=0),
    )(first, first_came, second, second_came)


def swap(value, axis, bit):
    count = lax.axis_size(axis)
    return lax.ppermute(value, axis, [(source, source ^ bit) for source in range(count)])


def inner_rows(left, right):
    return lax.dot_general(
        left, right, (((0,), (0,)), ((), ())), preferred_element_type=jnp.float32
    )


def doubled(held, bits):
    for bit in bits:
        held = held + [(mask ^ bit, swap(part, "dp", bit)) for mask, part in held]
    return held


def panel_blocks(held, data, dp, width):
    held = doubled(held, [1])
    held = [part for _, part in sorted(held, key=lambda pair: pair[0])]
    share, channels = held[0].shape[1:]
    if share == width:
        return held, data
    panel = jnp.zeros((2, channels, channels), held[0].dtype)
    for mask, part in enumerate(held):
        panel = lax.dynamic_update_slice(panel, part, (0, (data ^ mask) * share, 0))
    return [panel[:, at : at + width] for at in range(0, channels, width)], jnp.zeros_like(data)


def body(checkpoint, cotangent, depthwise, pointwise, genotype):
    micro, images, side = checkpoint.shape[1:4]
    channels = checkpoint.shape[5]
    rows = images * side * side
    dp = lax.axis_size("dp")
    sections = lax.axis_size("segment")
    pairs = sections // 2
    segment = lax.axis_index("segment")
    data = lax.axis_index("dp")
    half = segment % 2
    pair = segment // 2
    is_high = half == 1
    share = channels // dp
    width = 256
    mean_scale = 1.0 / (micro * images * dp)

    x_all = checkpoint[0].reshape(micro, rows, channels)
    x_own = lax.dynamic_index_in_dim(x_all, half, 0, keepdims=False)
    x_other = lax.dynamic_index_in_dim(x_all, 1 - half, 0, keepdims=False)
    kind_row = jnp.full((2, 1, channels), genotype[0].astype(jnp.float32))
    k_own = jnp.concatenate([depthwise[0], kind_row], axis=1)

    far_bits = [1 << bit for bit in range(dp.bit_length() - 2, 0, -1)]
    own_rows = jnp.swapaxes(pointwise[0], 0, 1)
    own_held = doubled([(0, own_rows)], far_bits)
    partner_rows, x_sent, k_sent = lax.optimization_barrier((swap(own_rows, "segment", 1), x_other, k_own))
    x_partner = swap(x_sent, "segment", 1)
    k_partner = swap(k_sent, "segment", 1)
    partner_held = doubled([(0, partner_rows)], far_bits)
    own_blocks, turned = panel_blocks(own_held, data, dp, width)
    scalars_own = jnp.stack([turned, genotype[0], genotype[0], half, pair]).astype(jnp.int32)
    first_own = forward_start(scalars_own, x_own, k_own, 0, side)
    hidden_own, slope_own, mixed_own = forward_rest(scalars_own, first_own, k_own, own_blocks, 0, side, True)
    upstream = lax.dynamic_index_in_dim(cotangent, half, 0, keepdims=False).reshape(rows, channels)
    x_partner, k_partner, slope_own, upstream = lax.optimization_barrier(
        (x_partner, k_partner, slope_own, upstream)
    )
    kind_partner = k_partner[0, TAPS, 0].astype(jnp.int32)
    scalars = jnp.stack([turned, genotype[0], kind_partner, half, pair]).astype(jnp.int32)
    first_partner = forward_start(scalars, x_partner, k_partner, 1, side)
    far, first_partner = lax.optimization_barrier(([part for _, part in partner_held], first_partner))
    partner_held = [(mask, part) for (mask, _), part in zip(partner_held, far)]
    partner_blocks, _ = panel_blocks(partner_held, data, dp, width)
    blocks = (own_blocks, partner_blocks)
    hidden_partner, slope_partner = forward_rest(
        scalars, first_partner, k_partner, partner_blocks, 1, side, False
    )

    xs, slopes, ks = (x_own, x_partner), (slope_own, slope_partner), (k_own, k_partner)
    state = ()
    for turn in range(pairs):
        source = pairs - 1 - turn
        if turn < pairs - 1:
            state, leaving = chain(scalars, upstream, xs, slopes, ks, blocks, state, source, (0, 1), side)
            upstream = lax.ppermute(
                leaving, "segment", [(2 * source + h, 2 * source - 2 + h) for h in range(2)]
            )
            if turn == 0:
                x_late, state = lax.optimization_barrier((x_other, state))
                first_other = forward_start(scalars_own, x_late, k_own, 0, side)
                _, _, mixed_other = forward_rest(
                    scalars_own, first_other, k_own, own_blocks, 0, side, True
                )
                state, first_other, mixed_other = lax.optimization_barrier((state, first_other, mixed_other))
        else:
            state, leaving = chain(scalars, upstream, xs, slopes, ks, blocks, state, source, (0,), side)
            up_own, up_partner = state[8:]
            up_other = swap(up_partner, "segment", 1)
            state, _ = chain(scalars, leaving, xs, slopes, ks, blocks, state[:8], source, (1,), side)

    in_own, in_partner, pre_own, pre_partner, mix_own, mix_partner, lin_own, lin_partner = state
    def products(left_own, left_other, right_own, right_other):
        def product(core):
            def rows_of(left):
                return jnp.concatenate(
                    [
                        lax.dynamic_slice(left, (0, (2 * at + core) * share), (rows, share))
                        for at in range(dp // 2)
                    ],
                    axis=1,
                )

            return inner_rows(rows_of(left_own), right_own) + inner_rows(rows_of(left_other), right_other)

        mine = data % 2
        return product(mine), swap(product(1 - mine).astype(jnp.bfloat16), "dp", 1)

    def halved(total, came, bit):
        def part(index):
            def pick(value):
                value = value.reshape(value.shape[:-2] + (2, -1, channels))
                return lax.dynamic_index_in_dim(value, index, value.ndim - 3, keepdims=False)

            return pick(total) + pick(came).astype(jnp.float32)

        mine = (data // bit) % 2
        return part(mine), part(1 - mine).astype(jnp.bfloat16)

    def scattered(stay, leave):
        bit = dp // 2
        while bit > 2:
            came = swap(leave, "dp", bit)
            bit //= 2
            stay, leave = halved(stay, came, bit)
        return stay.reshape(share, channels), swap(leave, "dp", bit).reshape(share, channels)

    sums_own = tap_sums(scalars, x_own, lin_own, hidden_own, mix_own, 0, side)
    sums_partner = tap_sums(scalars, x_partner, lin_partner, hidden_partner, mix_partner, 1, side)
    pre_other = swap(pre_partner, "segment", 1)
    up_other, sums_own, sums_partner = lax.optimization_barrier((up_other, sums_own, sums_partner))
    second = halved(*products(mixed_own, mixed_other, up_own, up_other), dp // 2)
    pre_other, in_partner = lax.optimization_barrier((pre_other, in_partner))
    in_other = swap(in_partner, "segment", 1)
    first = halved(*products(first_own, first_other, pre_own, pre_other), dp // 2)
    grad_point = joined(*scattered(*first), *scattered(*second), mean_scale)
    grad_input = jnp.where(is_high, jnp.stack([in_other, in_own]), jnp.stack([in_own, in_other]))

    total = sums_own + swap(sums_partner.astype(jnp.bfloat16), "segment", 1).astype(jnp.float32)
    bit = 1
    while bit < dp:
        sent = total.astype(jnp.bfloat16)
        total = sent.astype(jnp.float32) + swap(sent, "dp", bit).astype(jnp.float32)
        bit *= 2
    grad_depth = total * mean_scale

    return (
        grad_input.reshape(checkpoint.shape),
        grad_point[None],
        grad_depth[None],
    )


def solution(mesh):
    placed = (
        P("segment", None, "dp", None, None, None),
        P(None, "dp", None, None, None),
        P("segment", None, None, None),
        P("segment", "dp", None, None),
        P("segment"),
    )
    return jax.shard_map(
        body,
        mesh=mesh,
        in_specs=placed,
        out_specs=(
            P("segment", None, "dp", None, None, None),
            P("segment", "dp", None, None),
            P("segment", None, None, None),
        ),
        check_vma=False,
    )
```

```python
import functools

import jax
import jax.numpy as jnp
from jax import lax
from jax.experimental import pallas as pl
from jax.experimental.pallas import tpu as pltpu
from jax.sharding import PartitionSpec as P

LANES = 128
TAPS = 25
KEPT = (
    [(r, c) for r in (-1, 0, 1) for c in (-1, 0, 1)],
    [(r, c) for r in (-2, -1, 0, 1, 2) for c in (-2, -1, 0, 1, 2)],
    [(r, c) for r in (-2, 0, 2) for c in (-2, 0, 2)],
)
MIB = 2**20


def moved(value, step):
    if step == 0:
        return value
    side = value.shape[0]
    place = lax.broadcasted_iota(jnp.int32, value.shape, 0) + step
    return jnp.where((place >= 0) & (place < side), pltpu.roll(value, (-step) % side, 0), 0.0)


def conv(source, taps, kind, emit):
    side = source.shape[1]

    def run(kept):
        cols = sorted({c for _, c in kept})
        lines = sorted({r for r, _ in kept})

        def lane(chunk, carry):
            lanes = pl.ds(pl.multiple_of(chunk * LANES, LANES), LANES)
            weight = {(r, c): taps(5 * (r + 2) + c + 2, lanes) for r, c in kept}

            def row(p, carry):
                near = {r: source[p + r + 2, :, lanes] for r in lines}
                total = None
                for c in cols:
                    column = None
                    for r in lines:
                        term = weight[r, c] * near[r]
                        column = term if column is None else column + term
                    column = moved(column, c)
                    total = column if total is None else total + column
                emit(pl.ds(pl.multiple_of(p * side, side), side), lanes, total)
                return carry

            lax.fori_loop(0, side, row, 0, unroll=16)
            return carry

        lax.fori_loop(0, source.shape[2] // LANES, lane, 0)

    for which in range(3):
        pl.when(kind == which)(functools.partial(run, KEPT[which]))


def clear_edges(source):
    side = source.shape[1]
    zero = jnp.zeros((2,) + source.shape[1:], jnp.float32)
    source[:2] = zero
    source[side + 2 :] = zero


def chain_kernel(scalars, *refs, pair, visits, parts, aliased, side):
    up_in = refs[0]
    xs, slopes, ks = refs[1:3], refs[3:5], refs[5:7]
    blocks = (refs[7 : 7 + parts], refs[7 + parts : 7 + 2 * parts])
    at = 7 + 2 * parts + aliased
    held = 4 if visits[0] else 5
    outs = [refs[at + 2 * i : at + 2 * i + 2] for i in range(held)]
    in_out, pre_out, mix_out, lin_out = outs[:4]
    leave = refs[at + 2 * held]
    panels, factor, k_at, left_at, flat_at, source, came, went = refs[at + 2 * held + 1 :]
    width = panels.shape[1] // parts
    steps = 2 * len(visits)

    def piece(step, part):
        return panels.at[step, pl.ds(part * width, width)], came.at[step * (parts + 1) + part]

    def other(step):
        return factor.at[step], came.at[step * (parts + 1) + parts]

    def taps_of(visit):
        return k_at.at[visit], came.at[steps * (parts + 1) + visit]

    def fetch(step, order):
        slot = order[visits[step // 2]]
        stage = step % 2
        for part in range(parts):
            place, sem = piece(step, part)
            pltpu.make_async_copy(blocks[slot][part].at[1 - stage], place, sem).start()
        if stage == 0:
            place, sem = taps_of(step // 2)
            pltpu.make_async_copy(ks[slot], place, sem).start()
        place, sem = other(step)
        pltpu.make_async_copy((xs if stage else slopes)[slot], place, sem).start()

    def fetch_for(step):
        pl.when(scalars[3] == 1)(functools.partial(fetch, step, (0, 1)))
        pl.when(scalars[3] == 0)(functools.partial(fetch, step, (1, 0)))

    def send(value, outs, slot, sem):
        for which in range(2):
            pl.when(slot == which)(pltpu.make_async_copy(value, outs[which], went.at[sem]).start)

    def wait(place, sem):
        pltpu.make_async_copy(place, place, sem).wait()

    def go():
        first = pltpu.make_async_copy(up_in, left_at.at[0], came.at[steps * (parts + 1) + len(visits)])
        first.start()
        fetch_for(0)
        clear_edges(source)
        first.wait()

        def one(step, carry):
            index = step // 2
            stage = step % 2
            slot = (visits[0] + index) ^ (1 - scalars[3])
            left = left_at.at[step]
            for later in range(1, steps):
                pl.when(step == later - 1)(functools.partial(fetch_for, later))

            def multiply(part, carry):
                place, sem = piece(step, part)
                wait(place, sem)
                flat = lax.dot_general(
                    left[...], place[...], (((1,), (1,)), ((), ())), preferred_element_type=jnp.float32
                )
                wide = pl.ds(pl.multiple_of((scalars[0] ^ part) * width, LANES), width)
                flat_at[step, :, wide] = flat.astype(jnp.bfloat16)
                source[2 : side + 2, :, wide] = flat.reshape(side, side, width)
                return carry

            lax.fori_loop(0, parts, multiply, 0)

            @pl.when(stage == 0)
            def _():
                wait(*taps_of(index))
                if visits[0] == 0:
                    send(left, outs[4], slot, 3 * step)
                send(flat_at.at[step], mix_out, slot, 3 * step + 1)

            @pl.when(stage == 1)
            def _():
                send(flat_at.at[step], lin_out, slot, 3 * step + 1)

            wait(*other(step))
            result = left_at.at[step + 1]

            def taps(tap, lanes):
                return k_at[index, 1 - stage, TAPS - 1 - tap, lanes][None]

            def scaled(rows, lanes, total):
                slope = factor[step, rows, lanes].astype(jnp.float32)
                result[rows, lanes] = (total * slope).astype(jnp.bfloat16)

            def gated(rows, lanes, total):
                total = jnp.where(factor[step, rows, lanes].astype(jnp.float32) > 0, total, 0.0)
                base = left_at[2 * index, rows, lanes].astype(jnp.float32)
                result[rows, lanes] = (base + total).astype(jnp.bfloat16)

            for which, emit in enumerate((scaled, gated)):
                pl.when(stage == which)(functools.partial(conv, source, taps, scalars[1 + slot], emit))

            @pl.when(stage == 0)
            def _():
                send(result, pre_out, slot, 3 * step + 2)

            @pl.when(stage == 1)
            def _():
                send(result, in_out, slot, 3 * step + 2)
                if len(visits) == 1 and visits[0] == 0:
                    send(result, outs[4], 1 - slot, 3 * step)

            return carry

        lax.fori_loop(0, steps, one, 0)
        last = pltpu.make_async_copy(left_at.at[steps], leave, came.at[0])
        last.start()
        for step in range(steps):
            for which in range(3):
                if which > 0 or (step % 2 == 0 and visits[0] == 0) or visits == (0,):
                    wait(flat_at.at[0], went.at[3 * step + which])
        last.wait()

    pl.when(scalars[4] == pair)(go)


def chain(scalars, up, xs, slopes, ks, blocks, state, pair, visits, side):
    parts = len(blocks[0])
    rows, channels = up.shape
    steps = 2 * len(visits)
    flat = jax.ShapeDtypeStruct((rows, channels), jnp.bfloat16)
    anywhere = pl.BlockSpec(memory_space=pl.ANY)
    inputs = [up, *xs, *slopes, *ks, *blocks[0], *blocks[1], *state]
    first_state = 1 + len(inputs) - len(state)
    count = 8 if visits[0] else 10
    outs = pl.pallas_call(
        functools.partial(chain_kernel, pair=pair, visits=visits, parts=parts, aliased=len(state), side=side),
        in_specs=[pl.BlockSpec(memory_space=pltpu.SMEM)] + [anywhere] * len(inputs),
        out_specs=[anywhere] * (count + 1),
        out_shape=[flat] * (count + 1),
        input_output_aliases={first_state + i: i for i in range(len(state))},
        scratch_shapes=[
            pltpu.VMEM((steps, channels, channels), jnp.bfloat16),
            pltpu.VMEM((steps, rows, channels), jnp.bfloat16),
            pltpu.VMEM((len(visits),) + ks[0].shape, jnp.float32),
            pltpu.VMEM((steps + 1, rows, channels), jnp.bfloat16),
            pltpu.VMEM((steps, rows, channels), jnp.bfloat16),
            pltpu.VMEM((side + 4, side, channels), jnp.float32),
            pltpu.SemaphoreType.DMA((steps * (parts + 1) + len(visits) + 1,)),
            pltpu.SemaphoreType.DMA((3 * steps,)),
        ],
        compiler_params=pltpu.CompilerParams(vmem_limit_bytes=58 * MIB),
        cost_estimate=pl.CostEstimate(flops=10**10, bytes_accessed=12 * MIB, transcendentals=0),
    )(scalars, *inputs)
    return tuple(outs[:count]), outs[count]


def start_kernel(scalars, x, k, start, source, *, slot, side):
    clear_edges(source)
    source[2 : side + 2] = jnp.maximum(x[...].astype(jnp.float32), 0.0).reshape(side, side, x.shape[1])

    def emit(rows, lanes, total):
        start[rows, lanes] = total.astype(jnp.bfloat16)

    conv(source, lambda tap, lanes: k[0, tap, lanes][None], scalars[1 + slot], emit)


def rest_kernel(scalars, start, *refs, slot, side, parts, mixes):
    if mixes:
        k, *refs = refs
    blocks = refs[:parts]
    panel, came = refs[-2:]
    hidden, slope = refs[parts : parts + 2]
    width = blocks[0].shape[1]
    copies = [pltpu.make_async_copy(blocks[part].at[0], panel.at[part], came.at[part]) for part in range(parts)]
    for copy in copies:
        copy.start()
    if mixes:
        mixed, source = refs[parts + 2 : parts + 4]
        clear_edges(source)
    for copy in copies:
        copy.wait()

    def columns(part, carry):
        wide = pl.ds(pl.multiple_of(part * width, LANES), width)
        flat = None
        for inner in range(parts):
            below = pl.ds(pl.multiple_of((scalars[0] ^ inner) * width, LANES), width)
            term = jnp.dot(start[:, below], panel[inner, :, wide], preferred_element_type=jnp.float32)
            flat = term if flat is None else flat + term
        sigma = jax.nn.sigmoid(flat)
        rounded = (flat * sigma).astype(jnp.bfloat16)
        hidden[:, wide] = rounded
        slope[:, wide] = (sigma * (1.0 + flat * (1.0 - sigma))).astype(jnp.bfloat16)
        if mixes:
            source[2 : side + 2, :, wide] = rounded.astype(jnp.float32).reshape(side, side, width)
        return carry

    lax.fori_loop(0, parts, columns, 0)
    if mixes:

        def emit(rows, lanes, total):
            mixed[rows, lanes] = total.astype(jnp.bfloat16)

        conv(source, lambda tap, lanes: k[1, tap, lanes][None], scalars[1 + slot], emit)


SMEM = pl.BlockSpec(memory_space=pltpu.SMEM)
VMEM = pl.BlockSpec(memory_space=pltpu.VMEM)


def forward_start(scalars, x, k, slot, side):
    rows, channels = x.shape
    return pl.pallas_call(
        functools.partial(start_kernel, slot=slot, side=side),
        in_specs=[SMEM, VMEM, VMEM],
        out_specs=VMEM,
        out_shape=jax.ShapeDtypeStruct((rows, channels), jnp.bfloat16),
        scratch_shapes=[pltpu.VMEM((side + 4, side, channels), jnp.float32)],
        compiler_params=pltpu.CompilerParams(vmem_limit_bytes=58 * MIB),
        cost_estimate=pl.CostEstimate(flops=1, bytes_accessed=1, transcendentals=0),
    )(scalars, x, k)


def forward_rest(scalars, start, k, blocks, slot, side, mixes):
    parts = len(blocks)
    rows, channels = start.shape
    outs = 3 if mixes else 2
    return pl.pallas_call(
        functools.partial(rest_kernel, slot=slot, side=side, parts=parts, mixes=mixes),
        in_specs=[SMEM, VMEM] + [VMEM] * mixes + [pl.BlockSpec(memory_space=pl.ANY)] * parts,
        out_specs=[VMEM] * outs,
        out_shape=[jax.ShapeDtypeStruct((rows, channels), jnp.bfloat16)] * outs,
        scratch_shapes=([pltpu.VMEM((side + 4, side, channels), jnp.float32)] if mixes else [])
        + [pltpu.VMEM((parts, channels // parts, channels), jnp.bfloat16), pltpu.SemaphoreType.DMA((parts,))],
        compiler_params=pltpu.CompilerParams(vmem_limit_bytes=58 * MIB),
        cost_estimate=pl.CostEstimate(flops=1, bytes_accessed=1, transcendentals=0),
    )(scalars, start, *([k] if mixes else []), *blocks)


def taps_kernel(scalars, x, lin, hidden, mix, out, source, *, slot, side):
    channels = x.shape[1]
    clear_edges(source)
    out[...] = jnp.zeros_like(out)

    def run(kept):
        cols = sorted({c for _, c in kept})
        lines = sorted({r for r, _ in kept})
        for which, (value, grad) in enumerate(((x, lin), (hidden, mix))):

            def lane(chunk, carry):
                lanes = pl.ds(pl.multiple_of(chunk * LANES, LANES), LANES)
                flat = value[:, lanes].astype(jnp.float32)
                if which == 0:
                    flat = jnp.maximum(flat, 0.0)
                source[2 : side + 2] = flat.reshape(side, side, LANES)

                def row(p, sums):
                    rows = pl.ds(pl.multiple_of(p * side, side), side)
                    here = grad[rows, lanes].astype(jnp.float32)
                    shifted = {c: moved(here, -c) for c in cols}
                    near = {r: source[p + r + 2] for r in lines}
                    new = []
                    for old, (r, c) in zip(sums, kept):
                        term = near[r] * shifted[c]
                        new.append(old + (term[: side // 2] + term[side // 2 :]))
                    return tuple(new)

                blank = jnp.zeros((side // 2, LANES), jnp.float32)
                sums = lax.fori_loop(0, side, row, (blank,) * len(kept), unroll=4)
                for total, (r, c) in zip(sums, kept):
                    out[which, 5 * (r + 2) + c + 2, lanes] = jnp.sum(total, axis=0)
                return carry

            lax.fori_loop(0, channels // LANES, lane, 0)

    for kind in range(3):
        pl.when(scalars[1 + slot] == kind)(functools.partial(run, KEPT[kind]))


def tap_sums(scalars, x, lin, hidden, mix, slot, side):
    channels = x.shape[1]
    return pl.pallas_call(
        functools.partial(taps_kernel, slot=slot, side=side),
        in_specs=[SMEM] + [VMEM] * 4,
        out_specs=VMEM,
        out_shape=jax.ShapeDtypeStruct((2, TAPS, channels), jnp.float32),
        scratch_shapes=[pltpu.VMEM((side + 4, side, LANES), jnp.float32)],
        compiler_params=pltpu.CompilerParams(vmem_limit_bytes=58 * MIB),
        cost_estimate=pl.CostEstimate(flops=1, bytes_accessed=1, transcendentals=0),
    )(scalars, x, lin, hidden, mix)


def joined_kernel(first, first_came, second, second_came, out, *, scale):
    out[:, 0, :] = (first[...] + first_came[...].astype(jnp.float32)) * scale
    out[:, 1, :] = (second[...] + second_came[...].astype(jnp.float32)) * scale


def joined(first, first_came, second, second_came, scale):
    share, channels = first.shape
    return pl.pallas_call(
        functools.partial(joined_kernel, scale=scale),
        in_specs=[VMEM] * 4,
        out_specs=VMEM,
        out_shape=jax.ShapeDtypeStruct((share, 2, channels), jnp.float32),
        compiler_params=pltpu.CompilerParams(vmem_limit_bytes=24 * MIB),
        cost_estimate=pl.CostEstimate(flops=1, bytes_accessed=1, transcendentals=0),
    )(first, first_came, second, second_came)


def swap(value, axis, bit):
    count = lax.axis_size(axis)
    return lax.ppermute(value, axis, [(source, source ^ bit) for source in range(count)])


def inner_rows(left, right):
    return lax.dot_general(left, right, (((0,), (0,)), ((), ())), preferred_element_type=jnp.float32)


def products(lefts, right_own, right_other):
    leave = inner_rows(lefts[0], right_own) + inner_rows(lefts[1], right_other)
    return leave.astype(jnp.bfloat16), inner_rows(lefts[2], right_own) + inner_rows(lefts[3], right_other)


def doubled(held, bits):
    for bit in bits:
        held = held + [(mask ^ bit, swap(part, "dp", bit)) for mask, part in held]
    return held


def panel_blocks(held, data, dp, width):
    held = doubled(held, [1])
    held = [part for _, part in sorted(held, key=lambda pair: pair[0])]
    share, channels = held[0].shape[1:]
    if share == width:
        return held, data
    panel = jnp.zeros((2, channels, channels), held[0].dtype)
    for mask, part in enumerate(held):
        panel = lax.dynamic_update_slice(panel, part, (0, (data ^ mask) * share, 0))
    return [panel[:, at : at + width] for at in range(0, channels, width)], jnp.zeros_like(data)


def body(checkpoint, cotangent, depthwise, pointwise, genotype):
    micro, images, side = checkpoint.shape[1:4]
    channels = checkpoint.shape[5]
    rows = images * side * side
    dp = lax.axis_size("dp")
    sections = lax.axis_size("segment")
    pairs = sections // 2
    segment = lax.axis_index("segment")
    data = lax.axis_index("dp")
    half = segment % 2
    pair = segment // 2
    is_high = half == 1
    share = channels // dp
    width = 256
    mean_scale = 1.0 / (micro * images * dp)

    x_all = checkpoint[0].reshape(micro, rows, channels)
    x_own = lax.dynamic_index_in_dim(x_all, half, 0, keepdims=False)
    x_other = lax.dynamic_index_in_dim(x_all, 1 - half, 0, keepdims=False)
    kind_row = jnp.full((2, 1, channels), genotype[0].astype(jnp.float32))
    k_own = jnp.concatenate([depthwise[0], kind_row], axis=1)

    far_bits = [1 << bit for bit in range(dp.bit_length() - 2, 0, -1)]
    own_rows = jnp.swapaxes(pointwise[0], 0, 1)
    own_held = doubled([(0, own_rows)], far_bits)
    partner_rows, x_sent, k_sent = lax.optimization_barrier((swap(own_rows, "segment", 1), x_other, k_own))
    x_partner = swap(x_sent, "segment", 1)
    k_partner = swap(k_sent, "segment", 1)
    partner_held = doubled([(0, partner_rows)], far_bits)
    own_blocks, turned = panel_blocks(own_held, data, dp, width)
    scalars_own = jnp.stack([turned, genotype[0], genotype[0], half, pair]).astype(jnp.int32)
    first_own = forward_start(scalars_own, x_own, k_own, 0, side)
    hidden_own, slope_own, mixed_own = forward_rest(scalars_own, first_own, k_own, own_blocks, 0, side, True)
    upstream = lax.dynamic_index_in_dim(cotangent, half, 0, keepdims=False).reshape(rows, channels)
    x_partner, k_partner, slope_own, upstream = lax.optimization_barrier(
        (x_partner, k_partner, slope_own, upstream)
    )
    kind_partner = k_partner[0, TAPS, 0].astype(jnp.int32)
    scalars = jnp.stack([turned, genotype[0], kind_partner, half, pair]).astype(jnp.int32)
    first_partner = forward_start(scalars, x_partner, k_partner, 1, side)
    far, first_partner = lax.optimization_barrier(([part for _, part in partner_held], first_partner))
    partner_held = [(mask, part) for (mask, _), part in zip(partner_held, far)]
    partner_blocks, _ = panel_blocks(partner_held, data, dp, width)
    blocks = (own_blocks, partner_blocks)
    hidden_partner, slope_partner = forward_rest(
        scalars, first_partner, k_partner, partner_blocks, 1, side, False
    )

    xs, slopes, ks = (x_own, x_partner), (slope_own, slope_partner), (k_own, k_partner)
    state = ()

    def rows_of(left, core):
        return jnp.concatenate(
            [lax.dynamic_slice(left, (0, (2 * at + core) * share), (rows, share)) for at in range(dp // 2)],
            axis=1,
        )

    for turn in range(pairs):
        source = pairs - 1 - turn
        if turn < pairs - 1:
            state, leaving = chain(scalars, upstream, xs, slopes, ks, blocks, state, source, (0, 1), side)
            upstream = lax.ppermute(
                leaving, "segment", [(2 * source + h, 2 * source - 2 + h) for h in range(2)]
            )
            if turn == 0:
                x_late, state = lax.optimization_barrier((x_other, state))
                first_other = forward_start(scalars_own, x_late, k_own, 0, side)
                _, _, mixed_other = forward_rest(
                    scalars_own, first_other, k_own, own_blocks, 0, side, True
                )
                state, first_other, mixed_other = lax.optimization_barrier((state, first_other, mixed_other))
            if turn == min(1, pairs - 2):
                first_lefts, second_lefts = (
                    [rows_of(left, core) for core in (1 - data % 2, data % 2) for left in pair_of]
                    for pair_of in ((first_own, first_other), (mixed_own, mixed_other))
                )
                state, first_lefts, second_lefts = lax.optimization_barrier((state, first_lefts, second_lefts))
        else:
            state, leaving = chain(scalars, upstream, xs, slopes, ks, blocks, state, source, (0,), side)
            up_own, up_partner = state[8:]
            up_other = swap(up_partner, "segment", 1)
            state, _ = chain(scalars, leaving, xs, slopes, ks, blocks, state[:8], source, (1,), side)

    in_own, in_partner, pre_own, pre_partner, mix_own, mix_partner, lin_own, lin_partner = state
    def halved(total, came, bit):
        def part(index):
            def pick(value):
                value = value.reshape(value.shape[:-2] + (2, -1, channels))
                return lax.dynamic_index_in_dim(value, index, value.ndim - 3, keepdims=False)

            return pick(total) + pick(came).astype(jnp.float32)

        mine = (data // bit) % 2
        return part(mine), part(1 - mine).astype(jnp.bfloat16)

    def scattered(stay, leave):
        bit = dp // 2
        while bit > 2:
            came = swap(leave, "dp", bit)
            bit //= 2
            stay, leave = halved(stay, came, bit)
        return stay.reshape(share, channels), swap(leave, "dp", bit).reshape(share, channels)

    pre_other = swap(pre_partner, "segment", 1)
    leave, stay = products(second_lefts, up_own, up_other)
    stay, leave = halved(stay, swap(leave, "dp", 1), dp // 2)
    second = scattered(stay, leave)
    pre_other, in_partner = lax.optimization_barrier((pre_other, in_partner))
    in_other = swap(in_partner, "segment", 1)
    leave, stay = products(first_lefts, pre_own, pre_other)
    stay, leave = halved(stay, swap(leave, "dp", 1), dp // 2)
    lin_partner, leave = lax.optimization_barrier((lin_partner, leave))
    first = scattered(stay, leave)
    sums_partner = tap_sums(scalars, x_partner, lin_partner, hidden_partner, mix_partner, 1, side)
    grad_input = jnp.where(is_high, jnp.stack([in_other, in_own]), jnp.stack([in_own, in_other]))
    lin_own, second, grad_input = lax.optimization_barrier((lin_own, second, grad_input))
    sums_own = tap_sums(scalars, x_own, lin_own, hidden_own, mix_own, 0, side)

    total = sums_own + swap(sums_partner.astype(jnp.bfloat16), "segment", 1).astype(jnp.float32)
    bit = 1
    while bit < dp:
        sent = total.astype(jnp.bfloat16)
        total = sent.astype(jnp.float32) + swap(sent, "dp", bit).astype(jnp.float32)
        bit *= 2
    grad_depth = total * mean_scale
    grad_point = joined(*first, *second, mean_scale)

    return (
        grad_input.reshape(checkpoint.shape),
        grad_point[None],
        grad_depth[None],
    )


def solution(mesh):
    placed = (
        P("segment", None, "dp", None, None, None),
        P(None, "dp", None, None, None),
        P("segment", None, None, None),
        P("segment", "dp", None, None),
        P("segment"),
    )
    return jax.shard_map(
        body,
        mesh=mesh,
        in_specs=placed,
        out_specs=(
            P("segment", None, "dp", None, None, None),
            P("segment", "dp", None, None),
            P("segment", None, None, None),
        ),
        check_vma=False,
    )
```

```python
import functools

import jax
import jax.numpy as jnp
from jax import lax
from jax.experimental import pallas as pl
from jax.experimental.pallas import tpu as pltpu
from jax.sharding import PartitionSpec as P

LANES = 128
TAPS = 25
KEPT = (
    [(r, c) for r in (-1, 0, 1) for c in (-1, 0, 1)],
    [(r, c) for r in (-2, -1, 0, 1, 2) for c in (-2, -1, 0, 1, 2)],
    [(r, c) for r in (-2, 0, 2) for c in (-2, 0, 2)],
)
MIB = 2**20


def moved(value, step):
    if step == 0:
        return value
    side = value.shape[0]
    place = lax.broadcasted_iota(jnp.int32, value.shape, 0) + step
    return jnp.where((place >= 0) & (place < side), pltpu.roll(value, (-step) % side, 0), 0.0)


def conv(source, taps, kind, emit):
    side = source.shape[1]

    def run(kept):
        cols = sorted({c for _, c in kept})
        lines = sorted({r for r, _ in kept})

        def lane(chunk, carry):
            lanes = pl.ds(pl.multiple_of(chunk * LANES, LANES), LANES)
            weight = {(r, c): taps(5 * (r + 2) + c + 2, lanes) for r, c in kept}

            def row(p, carry):
                near = {r: source[p + r + 2, :, lanes] for r in lines}
                total = None
                for c in cols:
                    column = None
                    for r in lines:
                        term = weight[r, c] * near[r]
                        column = term if column is None else column + term
                    column = moved(column, c)
                    total = column if total is None else total + column
                emit(pl.ds(pl.multiple_of(p * side, side), side), lanes, total)
                return carry

            lax.fori_loop(0, side, row, 0, unroll=16)
            return carry

        lax.fori_loop(0, source.shape[2] // LANES, lane, 0)

    for which in range(3):
        pl.when(kind == which)(functools.partial(run, KEPT[which]))


def clear_edges(source):
    side = source.shape[1]
    zero = jnp.zeros((2,) + source.shape[1:], jnp.float32)
    source[:2] = zero
    source[side + 2 :] = zero


def chain_kernel(scalars, *refs, pair, visits, parts, aliased, side):
    up_in = refs[0]
    xs, slopes, ks = refs[1:3], refs[3:5], refs[5:7]
    blocks = (refs[7 : 7 + parts], refs[7 + parts : 7 + 2 * parts])
    at = 7 + 2 * parts + aliased
    held = 4 if visits[0] else 5
    outs = [refs[at + 2 * i : at + 2 * i + 2] for i in range(held)]
    in_out, pre_out, mix_out, lin_out = outs[:4]
    leave = refs[at + 2 * held]
    panels, factor, k_at, left_at, flat_at, source, came, went = refs[at + 2 * held + 1 :]
    width = panels.shape[1] // parts
    steps = 2 * len(visits)

    def piece(step, part):
        return panels.at[step, pl.ds(part * width, width)], came.at[step * (parts + 1) + part]

    def other(step):
        return factor.at[step], came.at[step * (parts + 1) + parts]

    def taps_of(visit):
        return k_at.at[visit], came.at[steps * (parts + 1) + visit]

    def fetch(step, order):
        slot = order[visits[step // 2]]
        stage = step % 2
        for part in range(parts):
            place, sem = piece(step, part)
            pltpu.make_async_copy(blocks[slot][part].at[1 - stage], place, sem).start()
        if stage == 0:
            place, sem = taps_of(step // 2)
            pltpu.make_async_copy(ks[slot], place, sem).start()
        place, sem = other(step)
        pltpu.make_async_copy((xs if stage else slopes)[slot], place, sem).start()

    def fetch_for(step):
        pl.when(scalars[3] == 1)(functools.partial(fetch, step, (0, 1)))
        pl.when(scalars[3] == 0)(functools.partial(fetch, step, (1, 0)))

    def send(value, outs, slot, sem):
        for which in range(2):
            pl.when(slot == which)(pltpu.make_async_copy(value, outs[which], went.at[sem]).start)

    def wait(place, sem):
        pltpu.make_async_copy(place, place, sem).wait()

    def go():
        first = pltpu.make_async_copy(up_in, left_at.at[0], came.at[steps * (parts + 1) + len(visits)])
        first.start()
        fetch_for(0)
        clear_edges(source)
        first.wait()

        def one(step, carry):
            index = step // 2
            stage = step % 2
            slot = (visits[0] + index) ^ (1 - scalars[3])
            left = left_at.at[step]
            for later in range(1, steps):
                pl.when(step == later - 1)(functools.partial(fetch_for, later))

            def multiply(part, carry):
                place, sem = piece(step, part)
                wait(place, sem)
                flat = lax.dot_general(
                    left[...], place[...], (((1,), (1,)), ((), ())), preferred_element_type=jnp.float32
                )
                wide = pl.ds(pl.multiple_of((scalars[0] ^ part) * width, LANES), width)
                flat_at[step, :, wide] = flat.astype(jnp.bfloat16)
                source[2 : side + 2, :, wide] = flat.reshape(side, side, width)
                return carry

            lax.fori_loop(0, parts, multiply, 0)

            @pl.when(stage == 0)
            def _():
                wait(*taps_of(index))
                if visits[0] == 0:
                    send(left, outs[4], slot, 3 * step)
                send(flat_at.at[step], mix_out, slot, 3 * step + 1)

            @pl.when(stage == 1)
            def _():
                send(flat_at.at[step], lin_out, slot, 3 * step + 1)

            wait(*other(step))
            result = left_at.at[step + 1]

            def taps(tap, lanes):
                return k_at[index, 1 - stage, TAPS - 1 - tap, lanes][None]

            def scaled(rows, lanes, total):
                slope = factor[step, rows, lanes].astype(jnp.float32)
                result[rows, lanes] = (total * slope).astype(jnp.bfloat16)

            def gated(rows, lanes, total):
                total = jnp.where(factor[step, rows, lanes].astype(jnp.float32) > 0, total, 0.0)
                base = left_at[2 * index, rows, lanes].astype(jnp.float32)
                result[rows, lanes] = (base + total).astype(jnp.bfloat16)

            for which, emit in enumerate((scaled, gated)):
                pl.when(stage == which)(functools.partial(conv, source, taps, scalars[1 + slot], emit))

            @pl.when(stage == 0)
            def _():
                send(result, pre_out, slot, 3 * step + 2)

            @pl.when(stage == 1)
            def _():
                send(result, in_out, slot, 3 * step + 2)
                if len(visits) == 1 and visits[0] == 0:
                    send(result, outs[4], 1 - slot, 3 * step)

            return carry

        lax.fori_loop(0, steps, one, 0)
        last = pltpu.make_async_copy(left_at.at[steps], leave, came.at[0])
        last.start()
        for step in range(steps):
            for which in range(3):
                if which > 0 or (step % 2 == 0 and visits[0] == 0) or visits == (0,):
                    wait(flat_at.at[0], went.at[3 * step + which])
        last.wait()

    pl.when(scalars[4] == pair)(go)


def chain(scalars, up, xs, slopes, ks, blocks, state, pair, visits, side):
    parts = len(blocks[0])
    rows, channels = up.shape
    steps = 2 * len(visits)
    flat = jax.ShapeDtypeStruct((rows, channels), jnp.bfloat16)
    anywhere = pl.BlockSpec(memory_space=pl.ANY)
    inputs = [up, *xs, *slopes, *ks, *blocks[0], *blocks[1], *state]
    first_state = 1 + len(inputs) - len(state)
    count = 8 if visits[0] else 10
    outs = pl.pallas_call(
        functools.partial(chain_kernel, pair=pair, visits=visits, parts=parts, aliased=len(state), side=side),
        in_specs=[pl.BlockSpec(memory_space=pltpu.SMEM)] + [anywhere] * len(inputs),
        out_specs=[anywhere] * (count + 1),
        out_shape=[flat] * (count + 1),
        input_output_aliases={first_state + i: i for i in range(len(state))},
        scratch_shapes=[
            pltpu.VMEM((steps, channels, channels), jnp.bfloat16),
            pltpu.VMEM((steps, rows, channels), jnp.bfloat16),
            pltpu.VMEM((len(visits),) + ks[0].shape, jnp.float32),
            pltpu.VMEM((steps + 1, rows, channels), jnp.bfloat16),
            pltpu.VMEM((steps, rows, channels), jnp.bfloat16),
            pltpu.VMEM((side + 4, side, channels), jnp.float32),
            pltpu.SemaphoreType.DMA((steps * (parts + 1) + len(visits) + 1,)),
            pltpu.SemaphoreType.DMA((3 * steps,)),
        ],
        compiler_params=pltpu.CompilerParams(vmem_limit_bytes=58 * MIB),
        cost_estimate=pl.CostEstimate(flops=10**10, bytes_accessed=12 * MIB, transcendentals=0),
    )(scalars, *inputs)
    return tuple(outs[:count]), outs[count]


def start_kernel(scalars, x, k, start, source, *, slot, side):
    clear_edges(source)
    source[2 : side + 2] = jnp.maximum(x[...].astype(jnp.float32), 0.0).reshape(side, side, x.shape[1])

    def emit(rows, lanes, total):
        start[rows, lanes] = total.astype(jnp.bfloat16)

    conv(source, lambda tap, lanes: k[0, tap, lanes][None], scalars[1 + slot], emit)


def rest_kernel(scalars, start, *refs, slot, side, parts, mixes):
    if mixes:
        k, *refs = refs
    blocks = refs[:parts]
    panel, came = refs[-2:]
    hidden, slope = refs[parts : parts + 2]
    width = blocks[0].shape[1]
    copies = [pltpu.make_async_copy(blocks[part].at[0], panel.at[part], came.at[part]) for part in range(parts)]
    for copy in copies:
        copy.start()
    if mixes:
        mixed, source = refs[parts + 2 : parts + 4]
        clear_edges(source)
    for copy in copies:
        copy.wait()

    def columns(part, carry):
        wide = pl.ds(pl.multiple_of(part * width, LANES), width)
        flat = None
        for inner in range(parts):
            below = pl.ds(pl.multiple_of((scalars[0] ^ inner) * width, LANES), width)
            term = jnp.dot(start[:, below], panel[inner, :, wide], preferred_element_type=jnp.float32)
            flat = term if flat is None else flat + term
        sigma = jax.nn.sigmoid(flat)
        rounded = (flat * sigma).astype(jnp.bfloat16)
        hidden[:, wide] = rounded
        slope[:, wide] = (sigma * (1.0 + flat * (1.0 - sigma))).astype(jnp.bfloat16)
        if mixes:
            source[2 : side + 2, :, wide] = rounded.astype(jnp.float32).reshape(side, side, width)
        return carry

    lax.fori_loop(0, parts, columns, 0)
    if mixes:

        def emit(rows, lanes, total):
            mixed[rows, lanes] = total.astype(jnp.bfloat16)

        conv(source, lambda tap, lanes: k[1, tap, lanes][None], scalars[1 + slot], emit)


SMEM = pl.BlockSpec(memory_space=pltpu.SMEM)
VMEM = pl.BlockSpec(memory_space=pltpu.VMEM)


def forward_start(scalars, x, k, slot, side):
    rows, channels = x.shape
    return pl.pallas_call(
        functools.partial(start_kernel, slot=slot, side=side),
        in_specs=[SMEM, VMEM, VMEM],
        out_specs=VMEM,
        out_shape=jax.ShapeDtypeStruct((rows, channels), jnp.bfloat16),
        scratch_shapes=[pltpu.VMEM((side + 4, side, channels), jnp.float32)],
        compiler_params=pltpu.CompilerParams(vmem_limit_bytes=58 * MIB),
        cost_estimate=pl.CostEstimate(flops=1, bytes_accessed=1, transcendentals=0),
    )(scalars, x, k)


def forward_rest(scalars, start, k, blocks, slot, side, mixes):
    parts = len(blocks)
    rows, channels = start.shape
    outs = 3 if mixes else 2
    return pl.pallas_call(
        functools.partial(rest_kernel, slot=slot, side=side, parts=parts, mixes=mixes),
        in_specs=[SMEM, VMEM] + [VMEM] * mixes + [pl.BlockSpec(memory_space=pl.ANY)] * parts,
        out_specs=[VMEM] * outs,
        out_shape=[jax.ShapeDtypeStruct((rows, channels), jnp.bfloat16)] * outs,
        scratch_shapes=([pltpu.VMEM((side + 4, side, channels), jnp.float32)] if mixes else [])
        + [pltpu.VMEM((parts, channels // parts, channels), jnp.bfloat16), pltpu.SemaphoreType.DMA((parts,))],
        compiler_params=pltpu.CompilerParams(vmem_limit_bytes=58 * MIB),
        cost_estimate=pl.CostEstimate(flops=1, bytes_accessed=1, transcendentals=0),
    )(scalars, start, *([k] if mixes else []), *blocks)


def taps_kernel(scalars, x, lin, hidden, mix, out, source, *, slot, side):
    channels = x.shape[1]
    clear_edges(source)
    out[...] = jnp.zeros_like(out)

    def run(kept):
        cols = sorted({c for _, c in kept})
        lines = sorted({r for r, _ in kept})
        for which, (value, grad) in enumerate(((x, lin), (hidden, mix))):

            def lane(chunk, carry):
                lanes = pl.ds(pl.multiple_of(chunk * LANES, LANES), LANES)
                flat = value[:, lanes].astype(jnp.float32)
                if which == 0:
                    flat = jnp.maximum(flat, 0.0)
                source[2 : side + 2] = flat.reshape(side, side, LANES)

                def row(p, sums):
                    rows = pl.ds(pl.multiple_of(p * side, side), side)
                    here = grad[rows, lanes].astype(jnp.float32)
                    shifted = {c: moved(here, -c) for c in cols}
                    near = {r: source[p + r + 2] for r in lines}
                    new = []
                    for old, (r, c) in zip(sums, kept):
                        term = near[r] * shifted[c]
                        new.append(old + (term[: side // 2] + term[side // 2 :]))
                    return tuple(new)

                blank = jnp.zeros((side // 2, LANES), jnp.float32)
                sums = lax.fori_loop(0, side, row, (blank,) * len(kept), unroll=4)
                for total, (r, c) in zip(sums, kept):
                    out[which, 5 * (r + 2) + c + 2, lanes] = jnp.sum(total, axis=0)
                return carry

            lax.fori_loop(0, channels // LANES, lane, 0)

    for kind in range(3):
        pl.when(scalars[1 + slot] == kind)(functools.partial(run, KEPT[kind]))


def tap_sums(scalars, x, lin, hidden, mix, slot, side):
    channels = x.shape[1]
    return pl.pallas_call(
        functools.partial(taps_kernel, slot=slot, side=side),
        in_specs=[SMEM] + [VMEM] * 4,
        out_specs=VMEM,
        out_shape=jax.ShapeDtypeStruct((2, TAPS, channels), jnp.float32),
        scratch_shapes=[pltpu.VMEM((side + 4, side, LANES), jnp.float32)],
        compiler_params=pltpu.CompilerParams(vmem_limit_bytes=58 * MIB),
        cost_estimate=pl.CostEstimate(flops=1, bytes_accessed=1, transcendentals=0),
    )(scalars, x, lin, hidden, mix)


def joined_kernel(first, first_came, second, second_came, out, *, scale):
    out[:, 0, :] = (first[...] + first_came[...].astype(jnp.float32)) * scale
    out[:, 1, :] = (second[...] + second_came[...].astype(jnp.float32)) * scale


def joined(first, first_came, second, second_came, scale):
    share, channels = first.shape
    return pl.pallas_call(
        functools.partial(joined_kernel, scale=scale),
        in_specs=[VMEM] * 4,
        out_specs=VMEM,
        out_shape=jax.ShapeDtypeStruct((share, 2, channels), jnp.float32),
        compiler_params=pltpu.CompilerParams(vmem_limit_bytes=24 * MIB),
        cost_estimate=pl.CostEstimate(flops=1, bytes_accessed=1, transcendentals=0),
    )(first, first_came, second, second_came)


def swap(value, axis, bit):
    count = lax.axis_size(axis)
    return lax.ppermute(value, axis, [(source, source ^ bit) for source in range(count)])


def inner_rows(left, right):
    return lax.dot_general(left, right, (((0,), (0,)), ((), ())), preferred_element_type=jnp.float32)


def products(lefts, right_own, right_other):
    leave = inner_rows(lefts[0], right_own) + inner_rows(lefts[1], right_other)
    return leave.astype(jnp.bfloat16), inner_rows(lefts[2], right_own) + inner_rows(lefts[3], right_other)


def doubled(held, bits):
    for bit in bits:
        held = held + [(mask ^ bit, swap(part, "dp", bit)) for mask, part in held]
    return held


def panel_blocks(held, data, dp, width):
    held = doubled(held, [1])
    held = [part for _, part in sorted(held, key=lambda pair: pair[0])]
    share, channels = held[0].shape[1:]
    if share == width:
        return held, data
    panel = jnp.zeros((2, channels, channels), held[0].dtype)
    for mask, part in enumerate(held):
        panel = lax.dynamic_update_slice(panel, part, (0, (data ^ mask) * share, 0))
    return [panel[:, at : at + width] for at in range(0, channels, width)], jnp.zeros_like(data)


def body(checkpoint, cotangent, depthwise, pointwise, genotype):
    micro, images, side = checkpoint.shape[1:4]
    channels = checkpoint.shape[5]
    rows = images * side * side
    dp = lax.axis_size("dp")
    sections = lax.axis_size("segment")
    pairs = sections // 2
    segment = lax.axis_index("segment")
    data = lax.axis_index("dp")
    half = segment % 2
    pair = segment // 2
    is_high = half == 1
    share = channels // dp
    width = 256
    mean_scale = 1.0 / (micro * images * dp)

    x_all = checkpoint[0].reshape(micro, rows, channels)
    x_own = lax.dynamic_index_in_dim(x_all, half, 0, keepdims=False)
    x_other = lax.dynamic_index_in_dim(x_all, 1 - half, 0, keepdims=False)
    k_own = depthwise[0]

    far_bits = [1 << bit for bit in range(dp.bit_length() - 2, 0, -1)]
    own_rows = jnp.swapaxes(pointwise[0], 0, 1)
    own_held = doubled([(0, own_rows)], far_bits)
    partner_rows, x_sent, k_sent, kind_partner = lax.optimization_barrier(
        (swap(own_rows, "segment", 1), x_other, k_own, swap(genotype, "segment", 1))
    )
    x_partner = swap(x_sent, "segment", 1)
    k_partner = swap(k_sent, "segment", 1)
    partner_held = doubled([(0, partner_rows)], far_bits)
    own_blocks, turned = panel_blocks(own_held, data, dp, width)
    scalars_own = jnp.stack([turned, genotype[0], genotype[0], half, pair]).astype(jnp.int32)
    first_own = forward_start(scalars_own, x_own, k_own, 0, side)
    hidden_own, slope_own, mixed_own = forward_rest(scalars_own, first_own, k_own, own_blocks, 0, side, True)
    upstream = lax.dynamic_index_in_dim(cotangent, half, 0, keepdims=False).reshape(rows, channels)
    scalars = jnp.stack([turned, genotype[0], kind_partner[0], half, pair]).astype(jnp.int32)
    x_partner, k_partner, slope_own, upstream, scalars = lax.optimization_barrier(
        (x_partner, k_partner, slope_own, upstream, scalars)
    )
    first_partner = forward_start(scalars, x_partner, k_partner, 1, side)
    far, first_partner = lax.optimization_barrier(([part for _, part in partner_held], first_partner))
    partner_held = [(mask, part) for (mask, _), part in zip(partner_held, far)]
    partner_blocks, _ = panel_blocks(partner_held, data, dp, width)
    blocks = (own_blocks, partner_blocks)
    hidden_partner, slope_partner = forward_rest(
        scalars, first_partner, k_partner, partner_blocks, 1, side, False
    )

    xs, slopes, ks = (x_own, x_partner), (slope_own, slope_partner), (k_own, k_partner)
    state = ()

    def rows_of(left, core):
        return jnp.concatenate(
            [lax.dynamic_slice(left, (0, (2 * at + core) * share), (rows, share)) for at in range(dp // 2)],
            axis=1,
        )

    for turn in range(pairs):
        source = pairs - 1 - turn
        if turn < pairs - 1:
            state, leaving = chain(scalars, upstream, xs, slopes, ks, blocks, state, source, (0, 1), side)
            upstream = lax.ppermute(
                leaving, "segment", [(2 * source + h, 2 * source - 2 + h) for h in range(2)]
            )
            if turn == 0:
                x_late, state = lax.optimization_barrier((x_other, state))
                first_other = forward_start(scalars_own, x_late, k_own, 0, side)
                _, _, mixed_other = forward_rest(
                    scalars_own, first_other, k_own, own_blocks, 0, side, True
                )
                state, first_other, mixed_other = lax.optimization_barrier((state, first_other, mixed_other))
            if turn == min(1, pairs - 2):
                first_lefts, second_lefts = (
                    [rows_of(left, core) for core in (1 - data % 2, data % 2) for left in pair_of]
                    for pair_of in ((first_own, first_other), (mixed_own, mixed_other))
                )
                state, first_lefts, second_lefts = lax.optimization_barrier((state, first_lefts, second_lefts))
        else:
            state, leaving = chain(scalars, upstream, xs, slopes, ks, blocks, state, source, (0,), side)
            up_own, up_partner = state[8:]
            up_other = swap(up_partner, "segment", 1)
            state, _ = chain(scalars, leaving, xs, slopes, ks, blocks, state[:8], source, (1,), side)

    in_own, in_partner, pre_own, pre_partner, mix_own, mix_partner, lin_own, lin_partner = state
    def halved(total, came, bit):
        def part(index):
            def pick(value):
                value = value.reshape(value.shape[:-2] + (2, -1, channels))
                return lax.dynamic_index_in_dim(value, index, value.ndim - 3, keepdims=False)

            return pick(total) + pick(came).astype(jnp.float32)

        mine = (data // bit) % 2
        return part(mine), part(1 - mine).astype(jnp.bfloat16)

    def scattered(stay, leave):
        bit = dp // 2
        while bit > 2:
            came = swap(leave, "dp", bit)
            bit //= 2
            stay, leave = halved(stay, came, bit)
        return stay.reshape(share, channels), swap(leave, "dp", bit).reshape(share, channels)

    pre_other = swap(pre_partner, "segment", 1)
    leave, stay = products(second_lefts, up_own, up_other)
    stay, leave = halved(stay, swap(leave, "dp", 1), dp // 2)
    second = scattered(stay, leave)
    pre_other, in_partner = lax.optimization_barrier((pre_other, in_partner))
    in_other = swap(in_partner, "segment", 1)
    leave, stay = products(first_lefts, pre_own, pre_other)
    stay, leave = halved(stay, swap(leave, "dp", 1), dp // 2)
    lin_partner, leave = lax.optimization_barrier((lin_partner, leave))
    first = scattered(stay, leave)
    sums_partner = tap_sums(scalars, x_partner, lin_partner, hidden_partner, mix_partner, 1, side)
    grad_input = jnp.where(is_high, jnp.stack([in_other, in_own]), jnp.stack([in_own, in_other]))
    lin_own, second, grad_input = lax.optimization_barrier((lin_own, second, grad_input))
    sums_own = tap_sums(scalars, x_own, lin_own, hidden_own, mix_own, 0, side)

    total = sums_own + swap(sums_partner.astype(jnp.bfloat16), "segment", 1).astype(jnp.float32)
    bit = 1
    while bit < dp:
        sent = total.astype(jnp.bfloat16)
        total = sent.astype(jnp.float32) + swap(sent, "dp", bit).astype(jnp.float32)
        bit *= 2
    grad_depth = total * mean_scale
    grad_point = joined(*first, *second, mean_scale)

    return (
        grad_input.reshape(checkpoint.shape),
        grad_point[None],
        grad_depth[None],
    )


def solution(mesh):
    placed = (
        P("segment", None, "dp", None, None, None),
        P(None, "dp", None, None, None),
        P("segment", None, None, None),
        P("segment", "dp", None, None),
        P("segment"),
    )
    return jax.shard_map(
        body,
        mesh=mesh,
        in_specs=placed,
        out_specs=(
            P("segment", None, "dp", None, None, None),
            P("segment", "dp", None, None),
            P("segment", None, None, None),
        ),
        check_vma=False,
    )
```

```python
import functools

import jax
import jax.numpy as jnp
from jax import lax
from jax.experimental import pallas as pl
from jax.experimental.pallas import tpu as pltpu
from jax.sharding import PartitionSpec as P

LANES = 128
TAPS = 25
KEPT = (
    [(r, c) for r in (-1, 0, 1) for c in (-1, 0, 1)],
    [(r, c) for r in (-2, -1, 0, 1, 2) for c in (-2, -1, 0, 1, 2)],
    [(r, c) for r in (-2, 0, 2) for c in (-2, 0, 2)],
)
MIB = 2**20


def moved(value, step):
    if step == 0:
        return value
    side = value.shape[0]
    place = lax.broadcasted_iota(jnp.int32, value.shape, 0) + step
    return jnp.where((place >= 0) & (place < side), pltpu.roll(value, (-step) % side, 0), 0.0)


def conv(source, taps, kind, emit):
    side = source.shape[1]

    def run(kept):
        cols = sorted({c for _, c in kept})
        lines = sorted({r for r, _ in kept})

        def lane(chunk, carry):
            lanes = pl.ds(pl.multiple_of(chunk * LANES, LANES), LANES)
            weight = {(r, c): taps(5 * (r + 2) + c + 2, lanes) for r, c in kept}

            def row(p, carry):
                near = {r: source[p + r + 2, :, lanes] for r in lines}
                total = None
                for c in cols:
                    column = None
                    for r in lines:
                        term = weight[r, c] * near[r]
                        column = term if column is None else column + term
                    column = moved(column, c)
                    total = column if total is None else total + column
                emit(pl.ds(pl.multiple_of(p * side, side), side), lanes, total)
                return carry

            lax.fori_loop(0, side, row, 0, unroll=16)
            return carry

        lax.fori_loop(0, source.shape[2] // LANES, lane, 0, unroll=2)

    for which in range(3):
        pl.when(kind == which)(functools.partial(run, KEPT[which]))


def clear_edges(source):
    side = source.shape[1]
    zero = jnp.zeros((2,) + source.shape[1:], jnp.float32)
    source[:2] = zero
    source[side + 2 :] = zero


def chain_kernel(scalars, *refs, pair, visits, parts, aliased, side):
    up_in = refs[0]
    xs, slopes, ks = refs[1:3], refs[3:5], refs[5:7]
    blocks = (refs[7 : 7 + parts], refs[7 + parts : 7 + 2 * parts])
    at = 7 + 2 * parts + aliased
    held = 4 if visits[0] else 5
    outs = [refs[at + 2 * i : at + 2 * i + 2] for i in range(held)]
    in_out, pre_out, mix_out, lin_out = outs[:4]
    leave = refs[at + 2 * held]
    panels, factor, k_at, left_at, flat_at, source, came, went = refs[at + 2 * held + 1 :]
    width = panels.shape[1] // parts
    steps = 2 * len(visits)

    def piece(step, part):
        return panels.at[step, pl.ds(part * width, width)], came.at[step * (parts + 1) + part]

    def other(step):
        return factor.at[step], came.at[step * (parts + 1) + parts]

    def taps_of(visit):
        return k_at.at[visit], came.at[steps * (parts + 1) + visit]

    def fetch(step, order):
        slot = order[visits[step // 2]]
        stage = step % 2
        for part in range(parts):
            place, sem = piece(step, part)
            pltpu.make_async_copy(blocks[slot][part].at[1 - stage], place, sem).start()
        if stage == 0:
            place, sem = taps_of(step // 2)
            pltpu.make_async_copy(ks[slot], place, sem).start()
        place, sem = other(step)
        pltpu.make_async_copy((xs if stage else slopes)[slot], place, sem).start()

    def fetch_for(step):
        pl.when(scalars[3] == 1)(functools.partial(fetch, step, (0, 1)))
        pl.when(scalars[3] == 0)(functools.partial(fetch, step, (1, 0)))

    def send(value, outs, slot, sem):
        for which in range(2):
            pl.when(slot == which)(pltpu.make_async_copy(value, outs[which], went.at[sem]).start)

    def wait(place, sem):
        pltpu.make_async_copy(place, place, sem).wait()

    def go():
        first = pltpu.make_async_copy(up_in, left_at.at[0], came.at[steps * (parts + 1) + len(visits)])
        first.start()
        fetch_for(0)
        clear_edges(source)
        first.wait()

        def one(step, carry):
            index = step // 2
            stage = step % 2
            slot = (visits[0] + index) ^ (1 - scalars[3])
            left = left_at.at[step]
            for later in range(1, steps):
                pl.when(step == later - 1)(functools.partial(fetch_for, later))

            def multiply(part, carry):
                place, sem = piece(step, part)
                wait(place, sem)
                flat = lax.dot_general(
                    left[...], place[...], (((1,), (1,)), ((), ())), preferred_element_type=jnp.float32
                )
                wide = pl.ds(pl.multiple_of((scalars[0] ^ part) * width, LANES), width)
                flat_at[step, :, wide] = flat.astype(jnp.bfloat16)
                source[2 : side + 2, :, wide] = flat.reshape(side, side, width)
                return carry

            lax.fori_loop(0, parts, multiply, 0)

            @pl.when(stage == 0)
            def _():
                wait(*taps_of(index))
                if visits[0] == 0:
                    send(left, outs[4], slot, 3 * step)
                send(flat_at.at[step], mix_out, slot, 3 * step + 1)

            @pl.when(stage == 1)
            def _():
                send(flat_at.at[step], lin_out, slot, 3 * step + 1)

            wait(*other(step))
            result = left_at.at[step + 1]

            def taps(tap, lanes):
                return k_at[index, 1 - stage, TAPS - 1 - tap, lanes][None]

            def scaled(rows, lanes, total):
                slope = factor[step, rows, lanes].astype(jnp.float32)
                result[rows, lanes] = (total * slope).astype(jnp.bfloat16)

            def gated(rows, lanes, total):
                total = jnp.where(factor[step, rows, lanes].astype(jnp.float32) > 0, total, 0.0)
                base = left_at[2 * index, rows, lanes].astype(jnp.float32)
                result[rows, lanes] = (base + total).astype(jnp.bfloat16)

            for which, emit in enumerate((scaled, gated)):
                pl.when(stage == which)(functools.partial(conv, source, taps, scalars[1 + slot], emit))

            @pl.when(stage == 0)
            def _():
                send(result, pre_out, slot, 3 * step + 2)

            @pl.when(stage == 1)
            def _():
                send(result, in_out, slot, 3 * step + 2)
                if len(visits) == 1 and visits[0] == 0:
                    send(result, outs[4], 1 - slot, 3 * step)

            return carry

        lax.fori_loop(0, steps, one, 0)
        last = pltpu.make_async_copy(left_at.at[steps], leave, came.at[0])
        last.start()
        for step in range(steps):
            for which in range(3):
                if which > 0 or (step % 2 == 0 and visits[0] == 0) or visits == (0,):
                    wait(flat_at.at[0], went.at[3 * step + which])
        last.wait()

    pl.when(scalars[4] == pair)(go)


def chain(scalars, up, xs, slopes, ks, blocks, state, pair, visits, side):
    parts = len(blocks[0])
    rows, channels = up.shape
    steps = 2 * len(visits)
    flat = jax.ShapeDtypeStruct((rows, channels), jnp.bfloat16)
    anywhere = pl.BlockSpec(memory_space=pl.ANY)
    inputs = [up, *xs, *slopes, *ks, *blocks[0], *blocks[1], *state]
    first_state = 1 + len(inputs) - len(state)
    count = 8 if visits[0] else 10
    outs = pl.pallas_call(
        functools.partial(chain_kernel, pair=pair, visits=visits, parts=parts, aliased=len(state), side=side),
        in_specs=[pl.BlockSpec(memory_space=pltpu.SMEM)] + [anywhere] * len(inputs),
        out_specs=[anywhere] * (count + 1),
        out_shape=[flat] * (count + 1),
        input_output_aliases={first_state + i: i for i in range(len(state))},
        scratch_shapes=[
            pltpu.VMEM((steps, channels, channels), jnp.bfloat16),
            pltpu.VMEM((steps, rows, channels), jnp.bfloat16),
            pltpu.VMEM((len(visits),) + ks[0].shape, jnp.float32),
            pltpu.VMEM((steps + 1, rows, channels), jnp.bfloat16),
            pltpu.VMEM((steps, rows, channels), jnp.bfloat16),
            pltpu.VMEM((side + 4, side, channels), jnp.float32),
            pltpu.SemaphoreType.DMA((steps * (parts + 1) + len(visits) + 1,)),
            pltpu.SemaphoreType.DMA((3 * steps,)),
        ],
        compiler_params=pltpu.CompilerParams(vmem_limit_bytes=58 * MIB),
        cost_estimate=pl.CostEstimate(flops=10**10, bytes_accessed=12 * MIB, transcendentals=0),
    )(scalars, *inputs)
    return tuple(outs[:count]), outs[count]


def start_kernel(scalars, x, k, start, source, *, slot, side):
    clear_edges(source)
    source[2 : side + 2] = jnp.maximum(x[...].astype(jnp.float32), 0.0).reshape(side, side, x.shape[1])

    def emit(rows, lanes, total):
        start[rows, lanes] = total.astype(jnp.bfloat16)

    conv(source, lambda tap, lanes: k[0, tap, lanes][None], scalars[1 + slot], emit)


def rest_kernel(scalars, start_in, *refs, slot, side, parts, mixes):
    if mixes:
        k, *refs = refs
    blocks = refs[:parts]
    start, panel, came = refs[-3:]
    hidden, slope = refs[parts : parts + 2]
    width = blocks[0].shape[1]
    copies = [pltpu.make_async_copy(blocks[part].at[0], panel.at[part], came.at[part]) for part in range(parts)]
    copies.append(pltpu.make_async_copy(start_in, start, came.at[parts]))
    for copy in copies:
        copy.start()
    if mixes:
        mixed, source = refs[parts + 2 : parts + 4]
        clear_edges(source)
    for copy in copies:
        copy.wait()

    def columns(part, carry):
        wide = pl.ds(pl.multiple_of(part * width, LANES), width)
        flat = None
        for inner in range(parts):
            below = pl.ds(pl.multiple_of((scalars[0] ^ inner) * width, LANES), width)
            term = jnp.dot(start[:, below], panel[inner, :, wide], preferred_element_type=jnp.float32)
            flat = term if flat is None else flat + term
        sigma = jax.nn.sigmoid(flat)
        rounded = (flat * sigma).astype(jnp.bfloat16)
        hidden[:, wide] = rounded
        slope[:, wide] = (sigma * (1.0 + flat * (1.0 - sigma))).astype(jnp.bfloat16)
        if mixes:
            source[2 : side + 2, :, wide] = rounded.astype(jnp.float32).reshape(side, side, width)
        return carry

    lax.fori_loop(0, parts, columns, 0)
    if mixes:

        def emit(rows, lanes, total):
            mixed[rows, lanes] = total.astype(jnp.bfloat16)

        conv(source, lambda tap, lanes: k[1, tap, lanes][None], scalars[1 + slot], emit)


SMEM = pl.BlockSpec(memory_space=pltpu.SMEM)
VMEM = pl.BlockSpec(memory_space=pltpu.VMEM)


def forward_start(scalars, x, k, slot, side):
    rows, channels = x.shape
    return pl.pallas_call(
        functools.partial(start_kernel, slot=slot, side=side),
        in_specs=[SMEM, VMEM, VMEM],
        out_specs=VMEM,
        out_shape=jax.ShapeDtypeStruct((rows, channels), jnp.bfloat16),
        scratch_shapes=[pltpu.VMEM((side + 4, side, channels), jnp.float32)],
        compiler_params=pltpu.CompilerParams(vmem_limit_bytes=58 * MIB),
        cost_estimate=pl.CostEstimate(flops=1, bytes_accessed=1, transcendentals=0),
    )(scalars, x, k)


def forward_rest(scalars, start, k, blocks, slot, side, mixes):
    parts = len(blocks)
    rows, channels = start.shape
    outs = 3 if mixes else 2
    return pl.pallas_call(
        functools.partial(rest_kernel, slot=slot, side=side, parts=parts, mixes=mixes),
        in_specs=[SMEM, pl.BlockSpec(memory_space=pl.ANY)] + [VMEM] * mixes + [pl.BlockSpec(memory_space=pl.ANY)] * parts,
        out_specs=[VMEM] * outs,
        out_shape=[jax.ShapeDtypeStruct((rows, channels), jnp.bfloat16)] * outs,
        scratch_shapes=([pltpu.VMEM((side + 4, side, channels), jnp.float32)] if mixes else [])
        + [
            pltpu.VMEM((rows, channels), jnp.bfloat16),
            pltpu.VMEM((parts, channels // parts, channels), jnp.bfloat16),
            pltpu.SemaphoreType.DMA((parts + 1,)),
        ],
        compiler_params=pltpu.CompilerParams(vmem_limit_bytes=58 * MIB),
        cost_estimate=pl.CostEstimate(flops=1, bytes_accessed=1, transcendentals=0),
    )(scalars, start, *([k] if mixes else []), *blocks)


def taps_kernel(scalars, x, lin, hidden, mix, out, source, *, slot, side):
    channels = x.shape[1]
    clear_edges(source)
    out[...] = jnp.zeros_like(out)

    def run(kept):
        cols = sorted({c for _, c in kept})
        lines = sorted({r for r, _ in kept})
        for which, (value, grad) in enumerate(((x, lin), (hidden, mix))):

            def lane(chunk, carry):
                lanes = pl.ds(pl.multiple_of(chunk * LANES, LANES), LANES)
                flat = value[:, lanes].astype(jnp.float32)
                if which == 0:
                    flat = jnp.maximum(flat, 0.0)
                source[2 : side + 2] = flat.reshape(side, side, LANES)

                def row(p, sums):
                    rows = pl.ds(pl.multiple_of(p * side, side), side)
                    here = grad[rows, lanes].astype(jnp.float32)
                    shifted = {c: moved(here, -c) for c in cols}
                    near = {r: source[p + r + 2] for r in lines}
                    new = []
                    for old, (r, c) in zip(sums, kept):
                        term = near[r] * shifted[c]
                        new.append(old + (term[: side // 2] + term[side // 2 :]))
                    return tuple(new)

                blank = jnp.zeros((side // 2, LANES), jnp.float32)
                sums = lax.fori_loop(0, side, row, (blank,) * len(kept), unroll=4)
                for total, (r, c) in zip(sums, kept):
                    out[which, 5 * (r + 2) + c + 2, lanes] = jnp.sum(total, axis=0)
                return carry

            lax.fori_loop(0, channels // LANES, lane, 0)

    for kind in range(3):
        pl.when(scalars[1 + slot] == kind)(functools.partial(run, KEPT[kind]))


def tap_sums(scalars, x, lin, hidden, mix, slot, side):
    channels = x.shape[1]
    return pl.pallas_call(
        functools.partial(taps_kernel, slot=slot, side=side),
        in_specs=[SMEM] + [VMEM] * 4,
        out_specs=VMEM,
        out_shape=jax.ShapeDtypeStruct((2, TAPS, channels), jnp.float32),
        scratch_shapes=[pltpu.VMEM((side + 4, side, LANES), jnp.float32)],
        compiler_params=pltpu.CompilerParams(vmem_limit_bytes=58 * MIB),
        cost_estimate=pl.CostEstimate(flops=1, bytes_accessed=1, transcendentals=0),
    )(scalars, x, lin, hidden, mix)


def joined_kernel(first, first_came, second, second_came, out, *, scale):
    out[:, 0, :] = (first[...] + first_came[...].astype(jnp.float32)) * scale
    out[:, 1, :] = (second[...] + second_came[...].astype(jnp.float32)) * scale


def joined(first, first_came, second, second_came, scale):
    share, channels = first.shape
    return pl.pallas_call(
        functools.partial(joined_kernel, scale=scale),
        in_specs=[VMEM] * 4,
        out_specs=VMEM,
        out_shape=jax.ShapeDtypeStruct((share, 2, channels), jnp.float32),
        compiler_params=pltpu.CompilerParams(vmem_limit_bytes=24 * MIB),
        cost_estimate=pl.CostEstimate(flops=1, bytes_accessed=1, transcendentals=0),
    )(first, first_came, second, second_came)


def swap(value, axis, bit):
    count = lax.axis_size(axis)
    return lax.ppermute(value, axis, [(source, source ^ bit) for source in range(count)])


def inner_rows(left, right):
    return lax.dot_general(left, right, (((0,), (0,)), ((), ())), preferred_element_type=jnp.float32)


def products(lefts, right_own, right_other):
    leave = inner_rows(lefts[0], right_own) + inner_rows(lefts[1], right_other)
    return leave.astype(jnp.bfloat16), inner_rows(lefts[2], right_own) + inner_rows(lefts[3], right_other)


def doubled(held, bits):
    for bit in bits:
        held = held + [(mask ^ bit, swap(part, "dp", bit)) for mask, part in held]
    return held


def panel_blocks(held, data, dp, width):
    held = doubled(held, [1])
    held = [part for _, part in sorted(held, key=lambda pair: pair[0])]
    share, channels = held[0].shape[1:]
    if share == width:
        return held, data
    panel = jnp.zeros((2, channels, channels), held[0].dtype)
    for mask, part in enumerate(held):
        panel = lax.dynamic_update_slice(panel, part, (0, (data ^ mask) * share, 0))
    return [panel[:, at : at + width] for at in range(0, channels, width)], jnp.zeros_like(data)


def body(checkpoint, cotangent, depthwise, pointwise, genotype):
    micro, images, side = checkpoint.shape[1:4]
    channels = checkpoint.shape[5]
    rows = images * side * side
    dp = lax.axis_size("dp")
    sections = lax.axis_size("segment")
    pairs = sections // 2
    segment = lax.axis_index("segment")
    data = lax.axis_index("dp")
    half = segment % 2
    pair = segment // 2
    is_high = half == 1
    share = channels // dp
    width = 256
    mean_scale = 1.0 / (micro * images * dp)

    x_all = checkpoint[0].reshape(micro, rows, channels)
    x_own = lax.dynamic_index_in_dim(x_all, half, 0, keepdims=False)
    x_other = lax.dynamic_index_in_dim(x_all, 1 - half, 0, keepdims=False)
    k_own = depthwise[0]

    far_bits = [1 << bit for bit in range(dp.bit_length() - 2, 0, -1)]
    own_rows = jnp.swapaxes(pointwise[0], 0, 1)
    own_held = doubled([(0, own_rows)], far_bits)
    partner_rows, x_sent, k_sent, kind_partner = lax.optimization_barrier(
        (swap(own_rows, "segment", 1), x_other, k_own, swap(genotype, "segment", 1))
    )
    x_partner = swap(x_sent, "segment", 1)
    k_partner = swap(k_sent, "segment", 1)
    partner_held = doubled([(0, partner_rows)], far_bits)
    own_blocks, turned = panel_blocks(own_held, data, dp, width)
    scalars_own = jnp.stack([turned, genotype[0], genotype[0], half, pair]).astype(jnp.int32)
    first_own = forward_start(scalars_own, x_own, k_own, 0, side)
    hidden_own, slope_own, mixed_own = forward_rest(scalars_own, first_own, k_own, own_blocks, 0, side, True)
    upstream = lax.dynamic_index_in_dim(cotangent, half, 0, keepdims=False).reshape(rows, channels)
    scalars = jnp.stack([turned, genotype[0], kind_partner[0], half, pair]).astype(jnp.int32)
    x_partner, k_partner, slope_own, upstream, scalars = lax.optimization_barrier(
        (x_partner, k_partner, slope_own, upstream, scalars)
    )
    first_partner = forward_start(scalars, x_partner, k_partner, 1, side)
    far, first_partner = lax.optimization_barrier(([part for _, part in partner_held], first_partner))
    partner_held = [(mask, part) for (mask, _), part in zip(partner_held, far)]
    partner_blocks, _ = panel_blocks(partner_held, data, dp, width)
    blocks = (own_blocks, partner_blocks)
    hidden_partner, slope_partner = forward_rest(
        scalars, first_partner, k_partner, partner_blocks, 1, side, False
    )

    xs, slopes, ks = (x_own, x_partner), (slope_own, slope_partner), (k_own, k_partner)
    state = ()

    def rows_of(left, core):
        return jnp.concatenate(
            [lax.dynamic_slice(left, (0, (2 * at + core) * share), (rows, share)) for at in range(dp // 2)],
            axis=1,
        )

    for turn in range(pairs):
        source = pairs - 1 - turn
        if turn < pairs - 1:
            state, leaving = chain(scalars, upstream, xs, slopes, ks, blocks, state, source, (0, 1), side)
            upstream = lax.ppermute(
                leaving, "segment", [(2 * source + h, 2 * source - 2 + h) for h in range(2)]
            )
            if turn == 0:
                x_late, state = lax.optimization_barrier((x_other, state))
                first_other = forward_start(scalars_own, x_late, k_own, 0, side)
                _, _, mixed_other = forward_rest(
                    scalars_own, first_other, k_own, own_blocks, 0, side, True
                )
                state, first_other, mixed_other = lax.optimization_barrier((state, first_other, mixed_other))
            if turn == min(1, pairs - 2):
                first_lefts, second_lefts = (
                    [rows_of(left, core) for core in (1 - data % 2, data % 2) for left in pair_of]
                    for pair_of in ((first_own, first_other), (mixed_own, mixed_other))
                )
                state, first_lefts, second_lefts = lax.optimization_barrier((state, first_lefts, second_lefts))
        else:
            state, leaving = chain(scalars, upstream, xs, slopes, ks, blocks, state, source, (0,), side)
            up_own, up_partner = state[8:]
            up_other = swap(up_partner, "segment", 1)
            state, _ = chain(scalars, leaving, xs, slopes, ks, blocks, state[:8], source, (1,), side)

    in_own, in_partner, pre_own, pre_partner, mix_own, mix_partner, lin_own, lin_partner = state
    def halved(total, came, bit):
        def part(index):
            def pick(value):
                value = value.reshape(value.shape[:-2] + (2, -1, channels))
                return lax.dynamic_index_in_dim(value, index, value.ndim - 3, keepdims=False)

            return pick(total) + pick(came).astype(jnp.float32)

        mine = (data // bit) % 2
        return part(mine), part(1 - mine).astype(jnp.bfloat16)

    def scattered(stay, leave):
        bit = dp // 2
        while bit > 2:
            came = swap(leave, "dp", bit)
            bit //= 2
            stay, leave = halved(stay, came, bit)
        return stay.reshape(share, channels), swap(leave, "dp", bit).reshape(share, channels)

    pre_other = swap(pre_partner, "segment", 1)
    leave, stay = products(second_lefts, up_own, up_other)
    stay, leave = halved(stay, swap(leave, "dp", 1), dp // 2)
    second = scattered(stay, leave)
    pre_other, in_partner = lax.optimization_barrier((pre_other, in_partner))
    in_other = swap(in_partner, "segment", 1)
    leave, stay = products(first_lefts, pre_own, pre_other)
    stay, leave = halved(stay, swap(leave, "dp", 1), dp // 2)
    lin_partner, leave = lax.optimization_barrier((lin_partner, leave))
    first = scattered(stay, leave)
    sums_partner = tap_sums(scalars, x_partner, lin_partner, hidden_partner, mix_partner, 1, side)
    grad_input = jnp.where(is_high, jnp.stack([in_other, in_own]), jnp.stack([in_own, in_other]))
    lin_own, second, grad_input = lax.optimization_barrier((lin_own, second, grad_input))
    sums_own = tap_sums(scalars, x_own, lin_own, hidden_own, mix_own, 0, side)

    total = sums_own + swap(sums_partner.astype(jnp.bfloat16), "segment", 1).astype(jnp.float32)
    bit = 1
    while bit < dp:
        sent = total.astype(jnp.bfloat16)
        total = sent.astype(jnp.float32) + swap(sent, "dp", bit).astype(jnp.float32)
        bit *= 2
    grad_depth = total * mean_scale
    grad_point = joined(*first, *second, mean_scale)

    return (
        grad_input.reshape(checkpoint.shape),
        grad_point[None],
        grad_depth[None],
    )


def solution(mesh):
    placed = (
        P("segment", None, "dp", None, None, None),
        P(None, "dp", None, None, None),
        P("segment", None, None, None),
        P("segment", "dp", None, None),
        P("segment"),
    )
    return jax.shard_map(
        body,
        mesh=mesh,
        in_specs=placed,
        out_specs=(
            P("segment", None, "dp", None, None, None),
            P("segment", "dp", None, None),
            P("segment", None, None, None),
        ),
        check_vma=False,
    )
```
